256 devices in a mesh: replica: 4 (over z_lo, core), fsdp: 64 (over y, z_hi, x).
Axes of the slice: x: 4, y: 4, z: 8 (z_hi: 4, z_lo: 2; z = z_hi * 2 + z_lo), core: 2. Of those that a mesh axis runs over, the one named last changes fastest.
Arguments:
- local_params: bfloat16 [4, 2048, 8192], P('replica', 'fsdp'), may hold values from -6 to 6
- anchor: bfloat16 [2048, 8192], P('fsdp'), may hold values from -6 to 6
- feedback: float32 [4, 2048, 8192], P('replica', 'fsdp'), may hold values from -4 to 4
- master: float32 [2048, 8192], P('fsdp', 'replica'), may hold values from -6 to 6
- momentum: float32 [2048, 8192], P('fsdp', 'replica'), may hold values from -6 to 6
- tokens: bfloat16 [4, 20480, 8192], P('replica', 'fsdp'), may hold values from -16 to 16
- key_weight: bfloat16 [4, 8192, 512], P('replica', 'fsdp'), may hold values from -0.0625 to 0.0625
- key_cotangent: bfloat16 [4, 20480, 512], P('replica', 'fsdp'), may hold values from -0.0390625 to 0.0390625
Outputs:
- master_new: float32 [2048, 8192], P('fsdp', 'replica')
- momentum_new: float32 [2048, 8192], P('fsdp', 'replica')
- anchor_new: bfloat16 [2048, 8192], P('fsdp')
- keys: bfloat16 [4, 20480, 512], P('replica', 'fsdp')
- key_grad: float32 [4, 8192, 512], P('replica', 'fsdp')
The draws below stay inside these ranges and needn't reach their ends.
All inputs are finite; a program needn't handle non-finite values.
Results may differ from the reference program's by a relative error of at most 0.013.
Values may be sent and summed in bfloat16 or wider, within the bound.
A program may use at most 128 MiB of HBM per device.

```python
import jax
import jax.numpy as jnp
from jax import lax

D = 8192
FW = 512
REPLICAS = 4
FRAG = 2048
TOKENS = 20480
N_REPLICA = 4


def raised(values, rng, source, target, shards_of, factor):
    owner, partner = [(jnp.arange(values.shape[position]) // (values.shape[position] // shards_of)).reshape([-1 if axis == position else 1 for axis in range(values.ndim)]) for position in (source, target)]
    chosen = jax.random.permutation(rng, shards_of)[partner]
    strong = (owner == chosen) | (owner == (partner + shards_of // 2) % shards_of)
    return jnp.where(strong, factor * values, values)


def steps_of(stream_key, dims, pieces, least, top_value):
    def one(position, blocks):
        draws = jax.random.uniform(jax.random.fold_in(jax.random.fold_in(stream_key, 6), position), (blocks,), jnp.float32, least / len(pieces), top_value / len(pieces))
        return jnp.repeat(jnp.exp(draws), dims[position] // blocks).reshape((-1,) + (1,) * (len(dims) - position - 1))

    gain = one(*pieces[0])
    for cut in pieces[1:]:
        gain = gain * one(*cut)
    return gain


def noise(rng, shape, width, bound, cuts=(), kind=jnp.bfloat16):
    drawn = width * jax.random.normal(rng, shape, jnp.float32)
    if cuts:
        drawn = drawn * steps_of(rng, shape, cuts, -0.22, 0.18)
    return jnp.clip(drawn, -bound, bound).astype(kind)


def gaussian_with(key, shape, spread, limit, pieces, heavy, held_as=jnp.bfloat16):
    drawn = spread * jax.random.normal(key, shape, jnp.float32)
    if pieces:
        drawn = drawn * steps_of(key, shape, pieces, -0.22, 0.18)
    return jnp.clip(raised(drawn, jax.random.fold_in(key, 3), *heavy), -limit, limit).astype(held_as)


def setup_inputs(seed: int = 0) -> dict:
    key_list = jax.random.split(jax.random.key(seed), 9)
    local_params = noise(key_list[0], (REPLICAS, FRAG, D), 1.0, 6.0, ((0, 4), (1, 64)))
    anchor = noise(key_list[1], (FRAG, D), 1.0, 6.0, ((0, 64),))
    feedback = noise(key_list[2], (REPLICAS, FRAG, D), 0.3, 4.0, ((0, 4), (1, 64)), jnp.float32)
    master = noise(key_list[3], (FRAG, D), 1.0, 6.0, ((0, 64), (1, 4)), jnp.float32)
    momentum = noise(key_list[4], (FRAG, D), 0.5, 6.0, ((0, 64), (1, 4)), jnp.float32)
    tokens = gaussian_with(key_list[5], (REPLICAS, TOKENS, D), 1.0, 16.0, ((0, 4), (1, 64)), (1, 2, 64, 4.0))
    key_weight = noise(key_list[6], (REPLICAS, D, FW), D ** -0.5, 0.0625, ((0, 4), (1, 64)))
    key_cotangent = noise(key_list[7], (REPLICAS, TOKENS, FW), TOKENS ** -0.5, 0.0390625, ((0, 4), (1, 64)))
    return {"local_params": local_params, "anchor": anchor, "feedback": feedback, "master": master, "momentum": momentum, "tokens": tokens, "key_weight": key_weight, "key_cotangent": key_cotangent}


LR = 0.7
MU = 0.9


def reference(local_params, anchor, feedback, master, momentum, tokens, key_weight, key_cotangent):
    anchor_wide = anchor.astype(jnp.float32)
    total = jnp.zeros(anchor.shape, jnp.float32)
    for index in range(N_REPLICA):
        corrected = (anchor_wide - local_params[index].astype(jnp.float32)) + feedback[index]
        packed = lax.optimization_barrier(corrected.astype(jnp.bfloat16))
        total = total + packed.astype(jnp.float32)
    outer_grad = total / N_REPLICA
    momentum_new = MU * momentum + outer_grad
    master_new = master - LR * (outer_grad + MU * momentum_new)
    anchor_new = master_new.astype(jnp.bfloat16)
    keys_list = []
    grad_list = []
    for index in range(N_REPLICA):
        keys_list.append(jnp.dot(tokens[index], key_weight[index], preferred_element_type=jnp.float32).astype(jnp.bfloat16))
        grad_list.append(jnp.dot(tokens[index].T, key_cotangent[index], preferred_element_type=jnp.float32))
    keys = jnp.stack(keys_list)
    key_grad = jnp.stack(grad_list)
    return (master_new, momentum_new, anchor_new, keys, key_grad)
```

```python
import functools

import jax
import jax.numpy as jnp
from jax import lax
from jax.experimental import pallas as pl
from jax.experimental.pallas import tpu as pltpu
from jax.sharding import PartitionSpec as P

LR = 0.7
MU = 0.9
MESH = pl.DeviceIdType.MESH
F32 = jnp.float32
BF16 = jnp.bfloat16
SIDE = 4
BLK = 128
MESSAGES = 150


def kernel(
    lp, an, fb, ms, mo, tk, kw, kc,
    ms_o, mo_o, an_o, keys_o, kg_o,
    W, T, RF, RN, RC, RF2, RN2, RC2, RF3, RN3, RC3,
    tok, cot, cotT, lpv, anv, fbv, msv, mov, pk, RP, AN, msn, mon, acc, keyv, kgv,
    ssem, rsem, lsem,
):
    r = lax.axis_index("replica")
    f = lax.axis_index("fsdp")
    y, z, x = f // 16, (f // 4) % 4, f % 4
    here = {"y": y, "z": z, "x": x}

    def turn(v, s):
        return lax.rem(v + (s % SIDE), SIDE)

    def device(axis, s):
        c = dict(here)
        c[axis] = turn(c[axis], s)
        return (r, (c["y"] * SIDE + c["z"]) * SIDE + c["x"])

    def peer(k):
        return (lax.rem(r + k, 4), f)

    local = []

    def bring(src, dst):
        copy = pltpu.make_async_copy(src, dst, lsem.at[len(local)])
        copy.start()
        local.append(copy)
        return copy

    got_w = [
        bring(kw.at[0, :, pl.ds((2 * d + h) * BLK, BLK)], W.at[y, x, h, d, z])
        for h in range(2) for d in range(2)
    ]
    got_cot = bring(kc.at[0], cot)
    wide = tok.shape[1] // SIDE
    got_tok = {}
    for s in (2, 1, 3, 0):
        cols = pl.ds(pl.multiple_of(turn(y, s) * wide, wide), wide)
        got_tok[s] = bring(tk.at[0, :, cols], tok.at[:, cols])
    got_outer = [bring(an, anv), bring(lp.at[0], lpv), bring(fb.at[0], fbv)]
    got_state = [bring(ms, msv), bring(mo, mov)]

    barrier = pltpu.get_barrier_semaphore()
    partners = [device(axis, s) for axis in "xyz" for s in (1, -1)] + [peer(k) for k in (1, 2, 3)]
    for partner in partners:
        pl.semaphore_signal(barrier, inc=1, device_id=partner, device_id_type=MESH)
    pl.semaphore_wait(barrier, len(partners))

    messages = []

    def send(src, dst, to):
        i = len(messages)
        m = pltpu.make_async_remote_copy(
            src_ref=src, dst_ref=dst, send_sem=ssem.at[i], recv_sem=rsem.at[i],
            device_id=to, device_id_type=MESH,
        )
        m.start()
        messages.append(m)
        return m

    A = ("y", "x")
    B = ("x", "y")
    sent = {}

    def spot(h, a, b):
        return (a, b) if h == 0 else (b, a)

    def z1():
        for c in got_w:
            c.wait()
        for s in (1, -1):
            src = W.at[y, x, :, :, z]
            sent["z1", s] = send(src, src, device("z", s))

    def z2():
        for s in (1, -1):
            sent["z1", s].wait_recv()
            src = W.at[y, x, :, 0 if s == 1 else 1, turn(z, -s)]
            sent["z2", s] = send(src, src, device("z", s))

    def z_end():
        for s in (1, -1):
            sent["z2", s].wait_recv()

    def a1(p):
        for h in range(2):
            for s in (1, -1):
                src = W.at[y, x, h, :, turn(z, p)]
                sent["a1", h, p, s] = send(src, src, device(A[h], s))

    def a2(p):
        for h in range(2):
            for s in (1, -1):
                sent["a1", h, p, s].wait_recv()
                yy, xx = spot(h, turn(here[A[h]], -s), here[B[h]])
                src = W.at[yy, xx, h, 0 if s == 1 else 1, turn(z, p)]
                sent["a2", h, p, s] = send(src, src, device(A[h], s))

    def a_end():
        for h in range(2):
            for p in range(4):
                for s in (1, -1):
                    sent["a2", h, p, s].wait_recv()

    def b1(k):
        for h in range(2):
            for s in (1, -1):
                yy, xx = spot(h, turn(here[A[h]], k), here[B[h]])
                src = W.at[yy, xx, h]
                sent["b1", h, k, s] = send(src, src, device(B[h], s))

    def b2(k):
        for h in range(2):
            for s in (1, -1):
                sent["b1", h, k, s].wait_recv()
                yy, xx = spot(h, turn(here[A[h]], k), turn(here[B[h]], -s))
                src = W.at[yy, xx, h, 0 if s == 1 else 1]
                sent["b2", h, k, s] = send(src, src, device(B[h], s))

    def b_end(k):
        for h in range(2):
            for s in (1, -1):
                sent["b2", h, k, s].wait_recv()

    def tokens_at(yy, zz, xx):
        col = pl.multiple_of(((yy * SIDE + zz) * SIDE + xx) * BLK, BLK)
        return tok[:, pl.ds(col, BLK)]

    def keys(k, j, first=False):
        for h in range(2):
            yy, xx = spot(h, turn(here[A[h]], k), turn(here[B[h]], j))
            left = jnp.concatenate([tokens_at(yy, zz, xx) for zz in range(SIDE)], axis=1)
            right = jnp.concatenate(
                [W[yy, xx, h, d].reshape(SIDE * BLK, BLK) for d in range(2)], axis=1
            )
            part = jnp.dot(left, right, preferred_element_type=F32)
            acc[h] = part if first else acc[h] + part

    def unit(dx, dy):
        if dy in got_tok:
            got_tok.pop(dy).wait()
        yy, xx = turn(y, dy), turn(x, dx)

        @pl.loop(0, 2)
        def _(pair):
            right = jnp.concatenate([tokens_at(yy, 2 * pair + i, xx) for i in range(2)], axis=1)
            res = jnp.dot(cotT[...], right, preferred_element_type=F32).astype(BF16)
            for d in range(2):
                for h in range(2):
                    q = 2 * d + h
                    for i in range(2):
                        T[yy, xx, h, d, 2 * pair + i] = res[
                            q * BLK:(q + 1) * BLK, i * BLK:(i + 1) * BLK
                        ]

    def add4(yy, xx, h, d, others):
        @pl.loop(0, SIDE)
        def _(zz):
            total = T[yy, xx, h, d, zz].astype(F32)
            for ref, lead in others:
                total = total + ref[(*lead, zz)].astype(F32)
            T[yy, xx, h, d, zz] = total.astype(BF16)

    def w(s):
        return 0 if s == 1 else 1

    def far1(h, k):
        a, b = turn(here[A[h]], k), here[B[h]]
        for s in (1, -1):
            yy, xx = spot(h, a, turn(b, 2))
            sent["f1", h, k, s] = send(T.at[yy, xx, h, w(s)], RF.at[h, w(s), a], device(B[h], s))

    def near1(h, k):
        a, b = turn(here[A[h]], k), here[B[h]]
        for s in (1, -1):
            yy, xx = spot(h, a, turn(b, s))
            sent["n1", h, k, s] = send(
                T.at[yy, xx, h, 1 - w(s)], RN.at[h, w(s), a], device(B[h], s)
            )

    def mid1(k):
        for h in range(2):
            a, b = turn(here[A[h]], k), here[B[h]]
            for s in (1, -1):
                yy, xx = spot(h, a, turn(b, s))
                sent["f1", h, k, s].wait_recv()
                add4(yy, xx, h, w(s), [(RF, (h, w(s), a))])
                sent["c1", h, k, s] = send(
                    T.at[yy, xx, h, w(s)], RC.at[h, w(s), a], device(B[h], s)
                )

    def end1(k):
        for h in range(2):
            a, b = turn(here[A[h]], k), here[B[h]]
            yy, xx = spot(h, a, b)
            for s in (1, -1):
                sent["n1", h, k, s].wait_recv()
                sent["c1", h, k, s].wait_recv()
            for s in (1, -1):
                add4(yy, xx, h, w(s), [(RC, (h, w(s), a)), (RN, (h, 1 - w(s), a))])

    def far2():
        for h in range(2):
            yy, xx = spot(h, turn(here[A[h]], 2), here[B[h]])
            for s in (1, -1):
                sent["f2", h, s] = send(T.at[yy, xx, h, w(s)], RF2.at[h, w(s)], device(A[h], s))

    def near2():
        for h in range(2):
            for s in (1, -1):
                yy, xx = spot(h, turn(here[A[h]], s), here[B[h]])
                sent["n2", h, s] = send(T.at[yy, xx, h, 1 - w(s)], RN2.at[h, w(s)], device(A[h], s))

    def mid2():
        for h in range(2):
            for s in (1, -1):
                yy, xx = spot(h, turn(here[A[h]], s), here[B[h]])
                sent["f2", h, s].wait_recv()
                add4(yy, xx, h, w(s), [(RF2, (h, w(s)))])
                sent["c2", h, s] = send(T.at[yy, xx, h, w(s)], RC2.at[h, w(s)], device(A[h], s))

    def end2():
        for h in range(2):
            for s in (1, -1):
                sent["n2", h, s].wait_recv()
                sent["c2", h, s].wait_recv()
            for s in (1, -1):
                add4(y, x, h, w(s), [(RC2, (h, w(s))), (RN2, (h, 1 - w(s)))])

    def start3():
        for h in range(2):
            for s in (1, -1):
                sent["f3", h, s] = send(
                    T.at[y, x, h, w(s), turn(z, 2)], RF3.at[h, w(s)], device("z", s)
                )
            for s in (1, -1):
                sent["n3", h, s] = send(
                    T.at[y, x, h, 1 - w(s), turn(z, s)], RN3.at[h, w(s)], device("z", s)
                )

    def mid3():
        for h in range(2):
            for s in (1, -1):
                sent["f3", h, s].wait_recv()
                zz = turn(z, s)
                T[y, x, h, w(s), zz] = (
                    T[y, x, h, w(s), zz].astype(F32) + RF3[h, w(s)].astype(F32)
                ).astype(BF16)
                sent["c3", h, s] = send(T.at[y, x, h, w(s), zz], RC3.at[h, w(s)], device("z", s))

    def end3():
        for h in range(2):
            for s in (1, -1):
                sent["n3", h, s].wait_recv()
                sent["c3", h, s].wait_recv()
            for s in (1, -1):
                d = w(s)
                total = (
                    T[y, x, h, d, z].astype(F32)
                    + RC3[h, d].astype(F32)
                    + RN3[h, 1 - d].astype(F32)
                )
                kgv[:, (2 * d + h) * BLK:(2 * d + h + 1) * BLK] = total.T

    own = msv.shape[1]

    def outer_send():
        for c in got_outer:
            c.wait()
        for j in range(4):
            cols = slice(j * own, (j + 1) * own)
            corrected = (anv[:, cols].astype(F32) - lpv[:, cols].astype(F32)) + fbv[:, cols]
            pk[j] = corrected.astype(BF16)
        for k in (1, 2, 3):
            sent["pk", k] = send(pk.at[lax.rem(r + k, 4)], RP.at[k - 1], peer(k))

    def outer_step():
        for c in got_state:
            c.wait()
        total = pk[r].astype(F32)
        for k in (1, 2, 3):
            sent["pk", k].wait_recv()
            total = total + RP[k - 1].astype(F32)
        outer_grad = total / 4
        momentum_new = MU * mov[...] + outer_grad
        master_new = msv[...] - LR * (outer_grad + MU * momentum_new)
        mon[...] = momentum_new
        msn[...] = master_new
        AN[r] = master_new.astype(BF16)
        for k in (1, 2, 3):
            sent["an", k] = send(AN.at[r], AN.at[r], peer(k))
        bring(mon, mo_o)
        bring(msn, ms_o)

    def outer_end():
        for k in (1, 2, 3):
            sent["an", k].wait_recv()
        for j in range(4):
            bring(AN.at[j], an_o.at[:, pl.ds(j * own, own)])

    z1()
    a1(0)
    got_cot.wait()
    cotT[...] = cot[...].T
    unit(2, 2)
    far1(0, 2)
    far1(1, 2)
    unit(2, 1)
    far1(0, 1)
    unit(1, 2)
    far1(1, 1)
    unit(2, 3)
    far1(0, 3)
    z2()
    a1(3)
    a1(1)
    unit(3, 2)
    far1(1, 3)
    unit(2, 0)
    far1(0, 0)
    unit(0, 2)
    far1(1, 0)
    near1(0, 2)
    near1(1, 2)
    z_end()
    a1(2)
    a2(0)
    outer_send()
    unit(1, 1)
    unit(3, 1)
    near1(0, 1)
    unit(1, 3)
    near1(1, 1)
    unit(3, 3)
    near1(0, 3)
    near1(1, 3)
    a2(3)
    a2(1)
    mid1(2)
    unit(1, 0)
    unit(3, 0)
    near1(0, 0)
    unit(0, 1)
    unit(0, 3)
    near1(1, 0)
    unit(0, 0)
    a2(2)
    outer_step()
    b1(0)
    mid1(1)
    mid1(3)
    mid1(0)
    a_end()
    b1(3)
    b1(1)
    end1(2)
    far2()
    end1(1)
    end1(3)
    near2()
    b1(2)
    mid2()
    end1(0)
    b2(0)
    outer_end()
    end2()
    start3()
    keys(0, 0, first=True)
    keys(1, 0)
    keys(3, 0)
    keys(2, 0)
    b2(3)
    mid3()
    keys(0, 1)
    keys(0, -1)
    b2(1)
    keys(3, 1)
    keys(3, -1)
    end3()
    bring(kgv, kg_o.at[0])
    b2(2)
    keys(1, 1)
    keys(1, -1)
    b_end(0)
    keys(0, 2)
    b_end(3)
    keys(3, 2)
    keys(2, 1)
    keys(2, -1)
    b_end(1)
    keys(1, 2)
    b_end(2)
    keys(2, 2)
    for h in range(2):
        for d in range(2):
            q = 2 * d + h
            keyv[:, q * BLK:(q + 1) * BLK] = acc[h, :, d * BLK:(d + 1) * BLK].astype(BF16)
    bring(keyv, keys_o.at[0])
    for m in messages:
        m.wait_send()
    waited = len(got_w) + 1 + 4 + len(got_outer) + len(got_state)
    for c in local[waited:]:
        c.wait()


def on_device(lp, an, fb, ms, mo, tk, kw, kc):
    rows, width = an.shape
    own = ms.shape[1]
    tokens, fw = kc.shape[1], kc.shape[2]
    anywhere = pl.BlockSpec(memory_space=pl.ANY)
    out = [
        jax.ShapeDtypeStruct(ms.shape, F32),
        jax.ShapeDtypeStruct(mo.shape, F32),
        jax.ShapeDtypeStruct(an.shape, BF16),
        jax.ShapeDtypeStruct((1, tokens, fw), BF16),
        jax.ShapeDtypeStruct((1, BLK, fw), F32),
    ]
    blocks = (SIDE, SIDE, 2, 2, SIDE, BLK, BLK)
    v = pltpu.VMEM
    scratch = [
        v(blocks, BF16),
        v(blocks, BF16),
        *[v((2, 2, SIDE, SIDE, BLK, BLK), BF16)] * 3,
        *[v((2, 2, SIDE, BLK, BLK), BF16)] * 3,
        *[v((2, 2, BLK, BLK), BF16)] * 3,
        v((tokens, width), BF16),
        v((tokens, fw), BF16),
        v((fw, tokens), BF16),
        v((rows, width), BF16),
        v((rows, width), BF16),
        v((rows, width), F32),
        v((rows, own), F32),
        v((rows, own), F32),
        v((4, rows, own), BF16),
        v((3, rows, own), BF16),
        v((4, rows, own), BF16),
        v((rows, own), F32),
        v((rows, own), F32),
        v((2, tokens, fw // 2), F32),
        v((tokens, fw), BF16),
        v((BLK, fw), F32),
        pltpu.SemaphoreType.DMA((MESSAGES,)),
        pltpu.SemaphoreType.DMA((MESSAGES,)),
        pltpu.SemaphoreType.DMA((32,)),
    ]
    return tuple(
        pl.pallas_call(
            kernel,
            out_shape=out,
            in_specs=[anywhere] * 8,
            out_specs=[anywhere] * 5,
            scratch_shapes=scratch,
            compiler_params=pltpu.CompilerParams(
                collective_id=0, has_side_effects=True, vmem_limit_bytes=60 * 1024 * 1024
            ),
            cost_estimate=pl.CostEstimate(
                flops=4 * tokens * width * fw, bytes_accessed=12 * 1024 * 1024, transcendentals=0
            ),
        )(lp, an, fb, ms, mo, tk, kw, kc)
    )


def solution(mesh):
    in_specs = (
        P("replica", "fsdp", None),
        P("fsdp", None),
        P("replica", "fsdp", None),
        P("fsdp", "replica"),
        P("fsdp", "replica"),
        P("replica", "fsdp", None),
        P("replica", "fsdp", None),
        P("replica", "fsdp", None),
    )
    out_specs = (
        P("fsdp", "replica"),
        P("fsdp", "replica"),
        P("fsdp", None),
        P("replica", "fsdp", None),
        P("replica", "fsdp", None),
    )
    return jax.shard_map(
        on_device, mesh=mesh, in_specs=in_specs, out_specs=out_specs, check_vma=False
    )
```

```python
import functools

import jax
import jax.numpy as jnp
from jax import lax
from jax.experimental import pallas as pl
from jax.experimental.pallas import tpu as pltpu
from jax.sharding import PartitionSpec as P

LR = 0.7
MU = 0.9
MESH = pl.DeviceIdType.MESH
F32 = jnp.float32
BF16 = jnp.bfloat16
SIDE = 4
BLK = 128
HALF = BLK // 2
MESSAGES = 144


def kernel(
    lp, an, fb, ms, mo, tk, kw, kc,
    ms_o, mo_o, an_o, keys_o, kg_o,
    X, SP, C, W, T, RF, RN, RC, RF3, RN3, RC3, KA, KS, KR,
    tok, lpv, anv, fbv, msv, mov, pk, RP, AN, msn, mon, keyv, kgv,
    ssem, rsem, lsem,
):
    r = lax.axis_index("replica")
    f = lax.axis_index("fsdp")
    y, z, x = f // 16, (f // 4) % 4, f % 4
    here = {"y": y, "z": z, "x": x}
    E = ("x", "y")
    O = ("y", "x")
    count = tok.shape[0]

    def turn(v, s):
        return lax.rem(v + (s % SIDE), SIDE)

    def device(axis, s):
        c = dict(here)
        c[axis] = turn(c[axis], s)
        return (r, (c["y"] * SIDE + c["z"]) * SIDE + c["x"])

    def peer(k):
        return (lax.rem(r + k, 4), f)

    def rows_of(e):
        return pl.ds(pl.multiple_of(e * count, count), count)

    def w(s):
        return 0 if s == 1 else 1

    local = []

    def bring(src, dst):
        copy = pltpu.make_async_copy(src, dst, lsem.at[len(local)])
        copy.start()
        local.append(copy)
        return copy

    got_w = [
        bring(kw.at[0, pl.ds(h * HALF + d * HALF // 2, HALF // 2)], W.at[h, z, here[O[h]], d])
        for h in range(2) for d in range(2)
    ]
    got_c = [bring(kc.at[0], C.at[h, rows_of(here[E[h]])]) for h in range(2)]
    got_tok = {}
    for k in (2, 1, 3, 0):
        got_tok[k] = []
        for yy in range(SIDE):
            col = pl.multiple_of((yy * SIDE + turn(z, k)) * SIDE * BLK, SIDE * BLK)
            cols = pl.ds(col, SIDE * BLK)
            got_tok[k].append(bring(tk.at[0, :, cols], tok.at[:, cols]))
    got_outer = [bring(an, anv), bring(lp.at[0], lpv), bring(fb.at[0], fbv)]
    got_state = [bring(ms, msv), bring(mo, mov)]
    waited = len(local)

    barrier = pltpu.get_barrier_semaphore()
    partners = (
        [device(axis, s) for axis in "xy" for s in (1, 2, 3)]
        + [device("z", s) for s in (1, 3)]
        + [peer(k) for k in (1, 2, 3)]
    )
    for partner in partners:
        pl.semaphore_signal(barrier, inc=1, device_id=partner, device_id_type=MESH)
    pl.semaphore_wait(barrier, len(partners))

    messages = []
    sent = {}

    def send(key, src, dst, to):
        i = len(messages)
        m = pltpu.make_async_remote_copy(
            src_ref=src, dst_ref=dst, send_sem=ssem.at[i], recv_sem=rsem.at[i],
            device_id=to, device_id_type=MESH,
        )
        m.start()
        messages.append(m)
        sent[key] = m

    def arrived(*key):
        sent[key].wait_recv()

    def c1():
        for h in range(2):
            for s in (1, -1):
                send(("c1", h, s), kc.at[0], C.at[h, rows_of(here[E[h]])], device(E[h], s))

    def c2():
        for h in range(2):
            for s in (1, -1):
                arrived("c1", h, s)
                first = turn(here[E[h]], -s) * count + w(s) * (count // 2)
                src = C.at[h, pl.ds(pl.multiple_of(first, count // 2), count // 2)]
                send(("c2", h, s), src, src, device(E[h], s))

    def c_end():
        for c in got_c:
            c.wait()
        for h in range(2):
            for s in (1, -1):
                arrived("c2", h, s)

    def w1():
        for c in got_w:
            c.wait()
        for h in range(2):
            src = W.at[h, z, here[O[h]]]
            for s in (1, 3, 2):
                send(("w1", h, s), src, src, device(O[h], s))

    def w2(p):
        for h in range(2):
            if p:
                arrived("w1", h, SIDE - p)
            src = W.at[h, z, turn(here[O[h]], p)]
            for s in (1, -1):
                send(("w2", h, p, s), src, src, device("z", s))

    def w3(p):
        for h in range(2):
            for s in (1, -1):
                arrived("w2", h, p, s)
                src = W.at[h, turn(z, -s), turn(here[O[h]], p), w(s)]
                send(("w3", h, p, s), src, src, device("z", s))

    def w_end():
        for h in range(2):
            for p in range(SIDE):
                for s in (1, -1):
                    arrived("w3", h, p, s)

    def pack(h, s, k):
        zz, e = turn(z, k), here[E[h]]
        ee = turn(e, s)
        for i in range(2):
            cols = []
            for oo in (2 * i, 2 * i + 1):
                yy, xx = (oo, ee) if h == 0 else (ee, oo)
                col = ((yy * SIDE + zz) * SIDE + xx) * BLK
                v = tok[:, pl.ds(pl.multiple_of(col, BLK), BLK)]
                cols.append(v[:, :HALF] if h == 0 else v[:, HALF:])
            both = jnp.concatenate(cols, axis=1)
            if s:
                SP[h, s - 1, k, :, i * BLK:(i + 1) * BLK] = both
            else:
                X[h, zz, rows_of(e), i * BLK:(i + 1) * BLK] = both

    def pack_all(k):
        for c in got_tok.pop(k):
            c.wait()
        for s in (2, 1, 3, 0):
            for h in range(2):
                pack(h, s, k)

    def share(k):
        for s in (2, 1, 3):
            for h in range(2):
                send(
                    ("x", h, s, k), SP.at[h, s - 1, k],
                    X.at[h, turn(z, k), rows_of(here[E[h]])], device(E[h], s),
                )

    def shared(h, k):
        for s in (1, 2, 3):
            arrived("x", h, s, k)

    def term(h, k):
        zz = turn(z, k)
        res = lax.dot_general(
            X[h, zz], C[h], (((0,), (0,)), ((), ())), preferred_element_type=F32
        ).astype(BF16)
        T[h, zz] = res.reshape(SIDE, 2, HALF // 2, res.shape[1])

    def far1(h, k):
        zz, o = turn(z, k), here[O[h]]
        for s in (1, -1):
            send(
                ("f1", h, k, s), T.at[h, zz, turn(o, 2), w(s)], RF.at[h, w(s), k],
                device(O[h], s),
            )

    def near1(h, k):
        zz, o = turn(z, k), here[O[h]]
        for s in (1, -1):
            send(
                ("n1", h, k, s), T.at[h, zz, turn(o, s), 1 - w(s)], RN.at[h, w(s), k],
                device(O[h], s),
            )

    def add(zz, h, o, d, others):
        total = T[h, zz, o, d].astype(F32)
        for part in others:
            total = total + part.astype(F32)
        T[h, zz, o, d] = total.astype(BF16)

    def mid1(h, k):
        zz, o = turn(z, k), here[O[h]]
        for s in (1, -1):
            arrived("f1", h, k, s)
            add(zz, h, turn(o, s), w(s), [RF[h, w(s), k]])
            send(
                ("c1", h, k, s), T.at[h, zz, turn(o, s), w(s)], RC.at[h, w(s), k],
                device(O[h], s),
            )

    def end1(h, k):
        zz, o = turn(z, k), here[O[h]]
        for s in (1, -1):
            arrived("n1", h, k, s)
            arrived("c1", h, k, s)
        for d in range(2):
            add(zz, h, o, d, [RC[h, d, k], RN[h, 1 - d, k]])

    def far3(h):
        for s in (1, -1):
            send(
                ("f3", h, s), T.at[h, turn(z, 2), here[O[h]], w(s)], RF3.at[h, w(s)],
                device("z", s),
            )

    def near3(h, s):
        send(
            ("n3", h, s), T.at[h, turn(z, s), here[O[h]], 1 - w(s)], RN3.at[h, w(s)],
            device("z", s),
        )

    def mid3(h, s):
        arrived("f3", h, s)
        add(turn(z, s), h, here[O[h]], w(s), [RF3[h, w(s)]])
        send(
            ("c3", h, s), T.at[h, turn(z, s), here[O[h]], w(s)], RC3.at[h, w(s)],
            device("z", s),
        )

    def end3(h):
        for s in (1, -1):
            arrived("n3", h, s)
            arrived("c3", h, s)
        for d in range(2):
            first = h * HALF + d * HALF // 2
            kgv[first:first + HALF // 2, :] = (
                T[h, z, here[O[h]], d].astype(F32)
                + RC3[h, d].astype(F32)
                + RN3[h, 1 - d].astype(F32)
            )

    def keys(h, s, ks, first, last):
        e = turn(here[E[h]], s)
        left = jnp.concatenate([X[h, turn(z, k), rows_of(e)] for k in ks], axis=1)
        right = jnp.concatenate(
            [W[h, turn(z, k)].reshape(2 * BLK, W.shape[-1]) for k in ks], axis=0
        )
        total = jnp.dot(left, right, preferred_element_type=F32)
        if not first:
            total = total + KA[h, s]
        if last and s:
            KS[h, s - 1] = total.astype(BF16)
            send(("k", h, s), KS.at[h, s - 1], KR.at[h, s - 1], device(E[h], s))
        else:
            KA[h, s] = total

    def keys_end():
        total = KA[0, 0] + KA[1, 0]
        for h in range(2):
            for s in (1, 3, 2):
                arrived("k", h, s)
                total = total + KR[h, s - 1].astype(F32)
        keyv[...] = total.astype(BF16)
        bring(keyv, keys_o.at[0])

    own = msv.shape[1]

    def outer_send():
        for c in got_outer:
            c.wait()
        for j in range(4):
            cols = slice(j * own, (j + 1) * own)
            corrected = (anv[:, cols].astype(F32) - lpv[:, cols].astype(F32)) + fbv[:, cols]
            pk[j] = corrected.astype(BF16)
        for k in (1, 2, 3):
            send(("pk", k), pk.at[lax.rem(r + k, 4)], RP.at[k - 1], peer(k))

    def outer_step():
        for c in got_state:
            c.wait()
        total = pk[r].astype(F32)
        for k in (1, 2, 3):
            arrived("pk", k)
            total = total + RP[k - 1].astype(F32)
        outer_grad = total / 4
        momentum_new = MU * mov[...] + outer_grad
        master_new = msv[...] - LR * (outer_grad + MU * momentum_new)
        mon[...] = momentum_new
        msn[...] = master_new
        AN[r] = master_new.astype(BF16)
        for k in (1, 2, 3):
            send(("an", k), AN.at[r], AN.at[r], peer(k))
        bring(mon, mo_o)
        bring(msn, ms_o)

    def outer_end():
        for k in (1, 2, 3):
            arrived("an", k)
        for j in range(4):
            bring(AN.at[j], an_o.at[:, pl.ds(j * own, own)])

    def both(step, *args):
        for h in range(2):
            step(h, *args)

    def terms(k):
        for h in range(2):
            term(h, k)
            far1(h, k)
            near1(h, k)

    w1()
    c1()
    pack_all(2)
    share(2)
    w2(0)
    pack_all(1)
    share(1)
    w2(1)
    w2(3)
    w2(2)
    c2()
    pack_all(3)
    share(3)
    w3(0)
    pack_all(0)
    share(0)
    outer_send()
    w3(1)
    c_end()
    both(shared, 2)
    terms(2)
    w3(3)
    both(shared, 1)
    terms(1)
    w3(2)
    outer_step()

    both(shared, 3)
    terms(3)
    w_end()
    for s in (2, 1, 3, 0):
        both(keys, s, (2, 1), True, False)
    both(shared, 0)
    terms(0)
    both(mid1, 2)
    both(mid1, 1)
    for s in (2, 1, 3):
        both(keys, s, (3, 0), False, True)

    both(mid1, 3)
    both(end1, 2)
    both(far3)
    both(end1, 1)
    both(near3, 1)
    both(mid3, 1)
    both(mid1, 0)
    both(end1, 3)
    both(near3, -1)
    both(mid3, -1)
    both(keys, 0, (3, 0), False, False)
    both(end1, 0)
    both(end3)
    bring(kgv, kg_o.at[0])
    outer_end()
    keys_end()
    for m in messages:
        m.wait_send()
    for c in local[waited:]:
        c.wait()


def hand_over(*refs):
    sources, results, held, sems = refs[:5], refs[5:10], refs[10:15], refs[15]
    inward = [pltpu.make_async_copy(a, b, sems.at[0, i]) for i, (a, b) in enumerate(zip(sources, held))]
    outward = [pltpu.make_async_copy(a, b, sems.at[1, i]) for i, (a, b) in enumerate(zip(held, results))]
    for c in inward:
        c.start()
    for c, o in zip(inward, outward):
        c.wait()
        o.start()
    for o in outward:
        o.wait()


def on_device(lp, an, fb, ms, mo, tk, kw, kc):
    rows, width = an.shape
    own = ms.shape[1]
    tokens, fw = kc.shape[1], kc.shape[2]
    anywhere = pl.BlockSpec(memory_space=pl.ANY)
    out = [
        jax.ShapeDtypeStruct(ms.shape, F32),
        jax.ShapeDtypeStruct(mo.shape, F32),
        jax.ShapeDtypeStruct(an.shape, BF16),
        jax.ShapeDtypeStruct((1, tokens, fw), BF16),
        jax.ShapeDtypeStruct((1, BLK, fw), F32),
    ]
    v = pltpu.VMEM
    piece = (HALF // 2, fw)
    scratch = [
        v((2, SIDE, SIDE * tokens, SIDE * HALF), BF16),
        v((2, SIDE - 1, SIDE, tokens, SIDE * HALF), BF16),
        v((2, SIDE * tokens, fw), BF16),
        *[v((2, SIDE, SIDE, 2, *piece), BF16)] * 2,
        *[v((2, 2, SIDE, *piece), BF16)] * 3,
        *[v((2, 2, *piece), BF16)] * 3,
        v((2, SIDE, tokens, fw), F32),
        *[v((2, SIDE - 1, tokens, fw), BF16)] * 2,
        v((tokens, width), BF16),
        v((rows, width), BF16),
        v((rows, width), BF16),
        v((rows, width), F32),
        v((rows, own), F32),
        v((rows, own), F32),
        v((4, rows, own), BF16),
        v((3, rows, own), BF16),
        v((4, rows, own), BF16),
        v((rows, own), F32),
        v((rows, own), F32),
        v((tokens, fw), BF16),
        v((BLK, fw), F32),
        pltpu.SemaphoreType.DMA((MESSAGES,)),
        pltpu.SemaphoreType.DMA((MESSAGES,)),
        pltpu.SemaphoreType.DMA((36,)),
    ]
    done = pl.pallas_call(
        kernel,
        out_shape=out,
        in_specs=[anywhere] * 8,
        out_specs=[anywhere] * 5,
        scratch_shapes=scratch,
        compiler_params=pltpu.CompilerParams(
            collective_id=0, has_side_effects=True, vmem_limit_bytes=60 * 1024 * 1024
        ),
        cost_estimate=pl.CostEstimate(
            flops=4 * tokens * width * fw, bytes_accessed=12 * 1024 * 1024, transcendentals=0
        ),
    )(lp, an, fb, ms, mo, tk, kw, kc)
    return tuple(
        pl.pallas_call(
            hand_over,
            out_shape=out,
            in_specs=[anywhere] * 5,
            out_specs=[anywhere] * 5,
            scratch_shapes=[*[v(o.shape, o.dtype) for o in out], pltpu.SemaphoreType.DMA((2, 5))],
        )(*done)
    )


def solution(mesh):
    in_specs = (
        P("replica", "fsdp", None),
        P("fsdp", None),
        P("replica", "fsdp", None),
        P("fsdp", "replica"),
        P("fsdp", "replica"),
        P("replica", "fsdp", None),
        P("replica", "fsdp", None),
        P("replica", "fsdp", None),
    )
    out_specs = (
        P("fsdp", "replica"),
        P("fsdp", "replica"),
        P("fsdp", None),
        P("replica", "fsdp", None),
        P("replica", "fsdp", None),
    )
    return jax.shard_map(
        on_device, mesh=mesh, in_specs=in_specs, out_specs=out_specs, check_vma=False
    )
```

```python
import functools

import jax
import jax.numpy as jnp
from jax import lax
from jax.experimental import pallas as pl
from jax.experimental.pallas import tpu as pltpu
from jax.sharding import PartitionSpec as P

LR = 0.7
MU = 0.9
MESH = pl.DeviceIdType.MESH
F32 = jnp.float32
BF16 = jnp.bfloat16
SIDE = 4
BLK = 128
HALF = BLK // 2
MESSAGES = 148


def kernel(
    lp, an, fb, ms, mo, tk, kw, kc,
    ms_o, mo_o, an_o, keys_o, kg_o,
    X, SP, C, W, T, RF, RN, RC, RF3, RN3, RC3, KA, KS, KF, KN, KC,
    tok, lpv, anv, fbv, msv, mov, pk, RP, AN,
    ssem, rsem, lsem,
):
    r = lax.axis_index("replica")
    f = lax.axis_index("fsdp")
    y, z, x = f // 16, (f // 4) % 4, f % 4
    here = {"y": y, "z": z, "x": x}
    E = ("x", "y")
    O = ("y", "x")
    count = tok.shape[0]

    def turn(v, s):
        return lax.rem(v + (s % SIDE), SIDE)

    def device(axis, s):
        c = dict(here)
        c[axis] = turn(c[axis], s)
        return (r, (c["y"] * SIDE + c["z"]) * SIDE + c["x"])

    def peer(k):
        return (lax.rem(r + k, 4), f)

    def rows_of(e):
        return pl.ds(pl.multiple_of(e * count, count), count)

    def w(s):
        return 0 if s == 1 else 1

    local = []

    def bring(src, dst):
        copy = pltpu.make_async_copy(src, dst, lsem.at[len(local)])
        copy.start()
        local.append(copy)
        return copy

    got_w = [
        bring(kw.at[0, pl.ds(h * HALF + d * HALF // 2, HALF // 2)], W.at[h, z, here[O[h]], d])
        for h in range(2) for d in range(2)
    ]
    got_c = [bring(kc.at[0], C.at[h, rows_of(here[E[h]])]) for h in range(2)]
    got_tok = {}
    for k in (2, 1, 3, 0):
        got_tok[k] = []
        for yy in range(SIDE):
            col = pl.multiple_of((yy * SIDE + turn(z, k)) * SIDE * BLK, SIDE * BLK)
            cols = pl.ds(col, SIDE * BLK)
            got_tok[k].append(bring(tk.at[0, :, cols], tok.at[:, cols]))
    got_outer = [bring(an, anv), bring(lp.at[0], lpv), bring(fb.at[0], fbv)]
    got_state = [bring(ms, msv), bring(mo, mov)]

    barrier = pltpu.get_barrier_semaphore()
    partners = (
        [device(axis, s) for axis in "xy" for s in (1, 2, 3)]
        + [device("z", s) for s in (1, 3)]
        + [peer(k) for k in (1, 2, 3)]
    )
    for partner in partners:
        pl.semaphore_signal(barrier, inc=1, device_id=partner, device_id_type=MESH)
    pl.semaphore_wait(barrier, len(partners))

    messages = []
    sent = {}

    def send(key, src, dst, to):
        i = len(messages)
        m = pltpu.make_async_remote_copy(
            src_ref=src, dst_ref=dst, send_sem=ssem.at[i], recv_sem=rsem.at[i],
            device_id=to, device_id_type=MESH,
        )
        m.start()
        messages.append(m)
        sent[key] = m

    def arrived(*key):
        sent[key].wait_recv()

    def c1():
        for h in range(2):
            for s in (1, -1):
                send(("c1", h, s), kc.at[0], C.at[h, rows_of(here[E[h]])], device(E[h], s))

    def c2():
        for h in range(2):
            for s in (1, -1):
                arrived("c1", h, s)
                first = turn(here[E[h]], -s) * count + w(s) * (count // 2)
                src = C.at[h, pl.ds(pl.multiple_of(first, count // 2), count // 2)]
                send(("c2", h, s), src, src, device(E[h], s))

    def c_end():
        for c in got_c:
            c.wait()
        for h in range(2):
            for s in (1, -1):
                arrived("c2", h, s)

    def w1():
        for c in got_w:
            c.wait()
        for h in range(2):
            src = W.at[h, z, here[O[h]]]
            for s in (1, 3, 2):
                send(("w1", h, s), src, src, device(O[h], s))

    def w2(p):
        for h in range(2):
            if p:
                arrived("w1", h, SIDE - p)
            src = W.at[h, z, turn(here[O[h]], p)]
            for s in (1, -1):
                send(("w2", h, p, s), src, src, device("z", s))

    def w3(p):
        for h in range(2):
            for s in (1, -1):
                arrived("w2", h, p, s)
                src = W.at[h, turn(z, -s), turn(here[O[h]], p), w(s)]
                send(("w3", h, p, s), src, src, device("z", s))

    def w_end():
        for h in range(2):
            for p in range(SIDE):
                for s in (1, -1):
                    arrived("w3", h, p, s)

    def pack(h, s, k):
        zz, e = turn(z, k), here[E[h]]
        ee = turn(e, s)
        for i in range(2):
            cols = []
            for oo in (2 * i, 2 * i + 1):
                yy, xx = (oo, ee) if h == 0 else (ee, oo)
                col = ((yy * SIDE + zz) * SIDE + xx) * BLK
                v = tok[:, pl.ds(pl.multiple_of(col, BLK), BLK)]
                cols.append(v[:, :HALF] if h == 0 else v[:, HALF:])
            both = jnp.concatenate(cols, axis=1)
            if s:
                SP[h, s - 1, k, :, i * BLK:(i + 1) * BLK] = both
            else:
                X[h, zz, rows_of(e), i * BLK:(i + 1) * BLK] = both

    def pack_all(k):
        for c in got_tok.pop(k):
            c.wait()
        for s in (2, 1, 3, 0):
            for h in range(2):
                pack(h, s, k)

    def share(k):
        for s in (2, 1, 3):
            for h in range(2):
                send(
                    ("x", h, s, k), SP.at[h, s - 1, k],
                    X.at[h, turn(z, k), rows_of(here[E[h]])], device(E[h], s),
                )

    def shared(h, k):
        for s in (1, 2, 3):
            arrived("x", h, s, k)

    def term(h, k):
        zz = turn(z, k)
        res = lax.dot_general(
            X[h, zz], C[h], (((0,), (0,)), ((), ())), preferred_element_type=F32
        ).astype(BF16)
        T[h, zz] = res.reshape(SIDE, 2, HALF // 2, res.shape[1])

    def far1(h, k):
        zz, o = turn(z, k), here[O[h]]
        for s in (1, -1):
            send(
                ("f1", h, k, s), T.at[h, zz, turn(o, 2), w(s)], RF.at[h, w(s), k],
                device(O[h], s),
            )

    def near1(h, k):
        zz, o = turn(z, k), here[O[h]]
        for s in (1, -1):
            send(
                ("n1", h, k, s), T.at[h, zz, turn(o, s), 1 - w(s)], RN.at[h, w(s), k],
                device(O[h], s),
            )

    def add(zz, h, o, d, others):
        total = T[h, zz, o, d].astype(F32)
        for part in others:
            total = total + part.astype(F32)
        T[h, zz, o, d] = total.astype(BF16)

    def mid1(h, k):
        zz, o = turn(z, k), here[O[h]]
        for s in (1, -1):
            arrived("f1", h, k, s)
            add(zz, h, turn(o, s), w(s), [RF[h, w(s), k]])
            send(
                ("c1", h, k, s), T.at[h, zz, turn(o, s), w(s)], RC.at[h, w(s), k],
                device(O[h], s),
            )

    def end1(h, k):
        zz, o = turn(z, k), here[O[h]]
        for s in (1, -1):
            arrived("n1", h, k, s)
            arrived("c1", h, k, s)
        for d in range(2):
            add(zz, h, o, d, [RC[h, d, k], RN[h, 1 - d, k]])

    def far3(h):
        for s in (1, -1):
            send(
                ("f3", h, s), T.at[h, turn(z, 2), here[O[h]], w(s)], RF3.at[h, w(s)],
                device("z", s),
            )

    def near3(h, s):
        send(
            ("n3", h, s), T.at[h, turn(z, s), here[O[h]], 1 - w(s)], RN3.at[h, w(s)],
            device("z", s),
        )

    def mid3(h, s):
        arrived("f3", h, s)
        add(turn(z, s), h, here[O[h]], w(s), [RF3[h, w(s)]])
        send(
            ("c3", h, s), T.at[h, turn(z, s), here[O[h]], w(s)], RC3.at[h, w(s)],
            device("z", s),
        )

    def end3(h):
        for s in (1, -1):
            arrived("n3", h, s)
            arrived("c3", h, s)
        for d in range(2):
            first = h * HALF + d * HALF // 2
            kg_o[0, first:first + HALF // 2, :] = (
                T[h, z, here[O[h]], d].astype(F32)
                + RC3[h, d].astype(F32)
                + RN3[h, 1 - d].astype(F32)
            )

    def keys(h, s, ks, first, last):
        e = turn(here[E[h]], s)
        left = jnp.concatenate([X[h, turn(z, k), rows_of(e)] for k in ks], axis=1)
        right = jnp.concatenate(
            [W[h, turn(z, k)].reshape(2 * BLK, W.shape[-1]) for k in ks], axis=0
        )
        total = jnp.dot(left, right, preferred_element_type=F32)
        if not first:
            total = total + KA[h, s]
        if not last or s == 0:
            KA[h, s] = total
            return
        step = count // 2
        KS[h, s - 1] = total.astype(BF16)
        if s == 2:
            for t in (1, -1):
                send(
                    ("kf", h, t), KS.at[h, 1, pl.ds(w(t) * step, step)], KF.at[h, w(t)],
                    device(E[h], t),
                )
        else:
            t = 1 if s == 1 else -1
            KA[h, s] = total
            send(
                ("kn", h, t), KS.at[h, s - 1, pl.ds((1 - w(t)) * step, step)], KN.at[h, w(t)],
                device(E[h], t),
            )

    def keys_mid(h):
        step = count // 2
        for t in (1, -1):
            s, rows = t % SIDE, pl.ds(w(t) * step, step)
            arrived("kf", h, t)
            KS[h, s - 1, rows] = (KA[h, s, rows] + KF[h, w(t)].astype(F32)).astype(BF16)
            send(("kc", h, t), KS.at[h, s - 1, rows], KC.at[h, w(t)], device(E[h], t))

    def keys_end():
        step = count // 2
        for h in range(2):
            for t in (1, -1):
                arrived("kn", h, t)
        for d in range(2):
            rows = pl.ds(d * step, step)
            total = KA[0, 0, rows] + KA[1, 0, rows]
            for h in range(2):
                arrived("kc", h, 1 - 2 * d)
                total = total + KN[h, 1 - d].astype(F32) + KC[h, d].astype(F32)
            keys_o[0, rows] = total.astype(BF16)

    own = msv.shape[1]

    def outer_send():
        for c in got_outer:
            c.wait()
        for j in range(4):
            cols = slice(j * own, (j + 1) * own)
            corrected = (anv[:, cols].astype(F32) - lpv[:, cols].astype(F32)) + fbv[:, cols]
            pk[j] = corrected.astype(BF16)
        for k in (1, 2, 3):
            send(("pk", k), pk.at[lax.rem(r + k, 4)], RP.at[k - 1], peer(k))

    def outer_step():
        for c in got_state:
            c.wait()
        total = pk[r].astype(F32)
        for k in (1, 2, 3):
            arrived("pk", k)
            total = total + RP[k - 1].astype(F32)
        outer_grad = total / 4
        momentum_new = MU * mov[...] + outer_grad
        master_new = msv[...] - LR * (outer_grad + MU * momentum_new)
        mo_o[...] = momentum_new
        ms_o[...] = master_new
        AN[r] = master_new.astype(BF16)
        for k in (1, 2, 3):
            send(("an", k), AN.at[r], AN.at[r], peer(k))

    def outer_end():
        for k in (1, 2, 3):
            arrived("an", k)
        for j in range(4):
            an_o[:, j * own:(j + 1) * own] = AN[j]

    def both(step, *args):
        for h in range(2):
            step(h, *args)

    def terms(k):
        for h in range(2):
            term(h, k)
            far1(h, k)
            near1(h, k)

    w1()
    c1()
    pack_all(2)
    share(2)
    w2(0)
    pack_all(1)
    share(1)
    w2(1)
    w2(3)
    w2(2)
    c2()
    pack_all(3)
    share(3)
    w3(0)
    pack_all(0)
    share(0)
    outer_send()
    w3(1)
    c_end()
    both(shared, 2)
    terms(2)
    w3(3)
    both(shared, 1)
    terms(1)
    w3(2)
    outer_step()

    both(shared, 3)
    terms(3)
    w_end()
    for s in (2, 1, 3, 0):
        both(keys, s, (2, 1), True, False)
    both(shared, 0)
    terms(0)
    both(mid1, 2)
    both(mid1, 1)
    for s in (2, 1, 3):
        both(keys, s, (3, 0), False, True)

    both(mid1, 3)
    both(end1, 2)
    both(far3)
    both(keys_mid)
    both(end1, 1)
    both(near3, 1)
    both(mid3, 1)
    both(mid1, 0)
    both(end1, 3)
    both(near3, -1)
    both(mid3, -1)
    both(keys, 0, (3, 0), False, False)
    both(end1, 0)
    both(end3)
    outer_end()
    keys_end()
    for m in messages:
        m.wait_send()


def hand_over(*refs):
    sources, results, sems = refs[:5], refs[5:10], refs[10]
    copies = [pltpu.make_async_copy(a, b, sems.at[i]) for i, (a, b) in enumerate(zip(sources, results))]
    for c in copies:
        c.start()
    for c in copies:
        c.wait()


def on_device(lp, an, fb, ms, mo, tk, kw, kc):
    rows, width = an.shape
    own = ms.shape[1]
    tokens, fw = kc.shape[1], kc.shape[2]
    anywhere = pl.BlockSpec(memory_space=pl.ANY)
    out = [
        jax.ShapeDtypeStruct(ms.shape, F32),
        jax.ShapeDtypeStruct(mo.shape, F32),
        jax.ShapeDtypeStruct(an.shape, BF16),
        jax.ShapeDtypeStruct((1, tokens, fw), BF16),
        jax.ShapeDtypeStruct((1, BLK, fw), F32),
    ]
    v = pltpu.VMEM
    piece = (HALF // 2, fw)
    scratch = [
        v((2, SIDE, SIDE * tokens, SIDE * HALF), BF16),
        v((2, SIDE - 1, SIDE, tokens, SIDE * HALF), BF16),
        v((2, SIDE * tokens, fw), BF16),
        *[v((2, SIDE, SIDE, 2, *piece), BF16)] * 2,
        *[v((2, 2, SIDE, *piece), BF16)] * 3,
        *[v((2, 2, *piece), BF16)] * 3,
        v((2, SIDE, tokens, fw), F32),
        v((2, SIDE - 1, tokens, fw), BF16),
        *[v((2, 2, tokens // 2, fw), BF16)] * 3,
        v((tokens, width), BF16),
        v((rows, width), BF16),
        v((rows, width), BF16),
        v((rows, width), F32),
        v((rows, own), F32),
        v((rows, own), F32),
        v((4, rows, own), BF16),
        v((3, rows, own), BF16),
        v((4, rows, own), BF16),
        pltpu.SemaphoreType.DMA((MESSAGES,)),
        pltpu.SemaphoreType.DMA((MESSAGES,)),
        pltpu.SemaphoreType.DMA((27,)),
    ]
    done = pl.pallas_call(
        kernel,
        out_shape=[v(o.shape, o.dtype) for o in out],
        in_specs=[anywhere] * 8,
        out_specs=[pl.BlockSpec(memory_space=pltpu.VMEM)] * 5,
        scratch_shapes=scratch,
        compiler_params=pltpu.CompilerParams(
            collective_id=0, has_side_effects=True, vmem_limit_bytes=60 * 1024 * 1024
        ),
        cost_estimate=pl.CostEstimate(
            flops=4 * tokens * width * fw, bytes_accessed=12 * 1024 * 1024, transcendentals=0
        ),
    )(lp, an, fb, ms, mo, tk, kw, kc)
    return tuple(
        pl.pallas_call(
            hand_over,
            out_shape=out,
            in_specs=[pl.BlockSpec(memory_space=pltpu.VMEM)] * 5,
            out_specs=[anywhere] * 5,
            scratch_shapes=[pltpu.SemaphoreType.DMA((5,))],
        )(*[pltpu.with_memory_space_constraint(o, pltpu.VMEM) for o in done])
    )


def solution(mesh):
    in_specs = (
        P("replica", "fsdp", None),
        P("fsdp", None),
        P("replica", "fsdp", None),
        P("fsdp", "replica"),
        P("fsdp", "replica"),
        P("replica", "fsdp", None),
        P("replica", "fsdp", None),
        P("replica", "fsdp", None),
    )
    out_specs = (
        P("fsdp", "replica"),
        P("fsdp", "replica"),
        P("fsdp", None),
        P("replica", "fsdp", None),
        P("replica", "fsdp", None),
    )
    return jax.shard_map(
        on_device, mesh=mesh, in_specs=in_specs, out_specs=out_specs, check_vma=False
    )
```

```python
import functools

import jax
import jax.numpy as jnp
from jax import lax
from jax.experimental import pallas as pl
from jax.experimental.pallas import tpu as pltpu
from jax.sharding import PartitionSpec as P

LR = 0.7
MU = 0.9
MESH = pl.DeviceIdType.MESH
F32 = jnp.float32
BF16 = jnp.bfloat16
SIDE = 4
BLK = 128
HALF = BLK // 2
MESSAGES = 148


def kernel(
    lp, an, fb, ms, mo, tk, kw, kc,
    ms_o, mo_o, an_o, keys_o, kg_o,
    X, SP, C, W, T, RF, RN, RC, RF3, RN3, RC3, KA, KS, KF, KN, KC,
    tok, lpv, anv, fbv, msv, mov, pk, RP, AN,
    ssem, rsem, lsem,
):
    r = lax.axis_index("replica")
    f = lax.axis_index("fsdp")
    y, z, x = f // 16, (f // 4) % 4, f % 4
    here = {"y": y, "z": z, "x": x}
    E = ("x", "y")
    O = ("y", "x")
    count = tok.shape[0]

    def turn(v, s):
        return lax.rem(v + (s % SIDE), SIDE)

    def device(axis, s):
        c = dict(here)
        c[axis] = turn(c[axis], s)
        return (r, (c["y"] * SIDE + c["z"]) * SIDE + c["x"])

    def peer(k):
        return (lax.rem(r + k, 4), f)

    def rows_of(e):
        return pl.ds(pl.multiple_of(e * count, count), count)

    def w(s):
        return 0 if s == 1 else 1

    barrier = pltpu.get_barrier_semaphore()
    partners = (
        [device(axis, s) for axis in "xy" for s in (1, 2, 3)]
        + [device("z", s) for s in (1, 3)]
        + [peer(k) for k in (1, 2, 3)]
    )
    for partner in partners:
        pl.semaphore_signal(barrier, inc=1, device_id=partner, device_id_type=MESH)

    local = []

    def bring(src, dst):
        copy = pltpu.make_async_copy(src, dst, lsem.at[len(local)])
        copy.start()
        local.append(copy)
        return copy

    got_w = [
        bring(kw.at[0, pl.ds(h * HALF + d * HALF // 2, HALF // 2)], W.at[h, z, here[O[h]], d])
        for h in range(2) for d in range(2)
    ]
    got_c = [bring(kc.at[0], C.at[h, rows_of(here[E[h]])]) for h in range(2)]
    got_tok = {}
    for k in (2, 1, 3, 0):
        got_tok[k] = []
        for yy in range(SIDE):
            col = pl.multiple_of((yy * SIDE + turn(z, k)) * SIDE * BLK, SIDE * BLK)
            cols = pl.ds(col, SIDE * BLK)
            got_tok[k].append(bring(tk.at[0, :, cols], tok.at[:, cols]))
    got_outer = [bring(an, anv), bring(lp.at[0], lpv), bring(fb.at[0], fbv)]
    got_state = [bring(ms, msv), bring(mo, mov)]

    pl.semaphore_wait(barrier, len(partners))

    messages = []
    sent = {}

    def send(key, src, dst, to):
        i = len(messages)
        m = pltpu.make_async_remote_copy(
            src_ref=src, dst_ref=dst, send_sem=ssem.at[i], recv_sem=rsem.at[i],
            device_id=to, device_id_type=MESH,
        )
        m.start()
        messages.append(m)
        sent[key] = m

    def arrived(*key):
        sent[key].wait_recv()

    drained = []

    def drain():
        for m in messages[len(drained):]:
            m.wait_send()
            drained.append(m)

    def c1():
        for h in range(2):
            for s in (1, -1):
                send(("c1", h, s), kc.at[0], C.at[h, rows_of(here[E[h]])], device(E[h], s))

    def c2():
        for h in range(2):
            for s in (1, -1):
                arrived("c1", h, s)
                first = turn(here[E[h]], -s) * count + w(s) * (count // 2)
                src = C.at[h, pl.ds(pl.multiple_of(first, count // 2), count // 2)]
                send(("c2", h, s), src, src, device(E[h], s))

    def c_end():
        for c in got_c:
            c.wait()
        for h in range(2):
            for s in (1, -1):
                arrived("c2", h, s)

    def w1():
        for c in got_w:
            c.wait()
        for h in range(2):
            src = W.at[h, z, here[O[h]]]
            for s in (1, 3, 2):
                send(("w1", h, s), src, src, device(O[h], s))

    def w2(p):
        for h in range(2):
            if p:
                arrived("w1", h, SIDE - p)
            src = W.at[h, z, turn(here[O[h]], p)]
            for s in (1, -1):
                send(("w2", h, p, s), src, src, device("z", s))

    def w3(p):
        for h in range(2):
            for s in (1, -1):
                arrived("w2", h, p, s)
                src = W.at[h, turn(z, -s), turn(here[O[h]], p), w(s)]
                send(("w3", h, p, s), src, src, device("z", s))

    def w_end():
        for h in range(2):
            for p in range(SIDE):
                for s in (1, -1):
                    arrived("w3", h, p, s)

    def pack(h, s, k):
        zz, e = turn(z, k), here[E[h]]
        ee = turn(e, s)
        for i in range(2):
            cols = []
            for oo in (2 * i, 2 * i + 1):
                yy, xx = (oo, ee) if h == 0 else (ee, oo)
                col = ((yy * SIDE + zz) * SIDE + xx) * BLK
                v = tok[:, pl.ds(pl.multiple_of(col, BLK), BLK)]
                cols.append(v[:, :HALF] if h == 0 else v[:, HALF:])
            both = jnp.concatenate(cols, axis=1)
            if s:
                SP[h, s - 1, k, :, i * BLK:(i + 1) * BLK] = both
            else:
                X[h, zz, rows_of(e), i * BLK:(i + 1) * BLK] = both

    def pack_all(k):
        for c in got_tok.pop(k):
            c.wait()
        for s in (2, 1, 3, 0):
            for h in range(2):
                pack(h, s, k)

    def share(k):
        for s in (2, 1, 3):
            for h in range(2):
                send(
                    ("x", h, s, k), SP.at[h, s - 1, k],
                    X.at[h, turn(z, k), rows_of(here[E[h]])], device(E[h], s),
                )

    def shared(h, k):
        for s in (1, 2, 3):
            arrived("x", h, s, k)

    def term(h, k):
        zz = turn(z, k)
        res = lax.dot_general(
            X[h, zz], C[h], (((0,), (0,)), ((), ())), preferred_element_type=F32
        ).astype(BF16)
        T[h, zz] = res.reshape(SIDE, 2, HALF // 2, res.shape[1])

    def far1(h, k):
        zz, o = turn(z, k), here[O[h]]
        for s in (1, -1):
            send(
                ("f1", h, k, s), T.at[h, zz, turn(o, 2), w(s)], RF.at[h, w(s), k],
                device(O[h], s),
            )

    def near1(h, k):
        zz, o = turn(z, k), here[O[h]]
        for s in (1, -1):
            send(
                ("n1", h, k, s), T.at[h, zz, turn(o, s), 1 - w(s)], RN.at[h, w(s), k],
                device(O[h], s),
            )

    def add(zz, h, o, d, others):
        total = T[h, zz, o, d].astype(F32)
        for part in others:
            total = total + part.astype(F32)
        T[h, zz, o, d] = total.astype(BF16)

    def mid1(h, k):
        zz, o = turn(z, k), here[O[h]]
        for s in (1, -1):
            arrived("f1", h, k, s)
            add(zz, h, turn(o, s), w(s), [RF[h, w(s), k]])
            send(
                ("c1", h, k, s), T.at[h, zz, turn(o, s), w(s)], RC.at[h, w(s), k],
                device(O[h], s),
            )

    def end1(h, k):
        zz, o = turn(z, k), here[O[h]]
        for s in (1, -1):
            arrived("n1", h, k, s)
            arrived("c1", h, k, s)
        for d in range(2):
            add(zz, h, o, d, [RC[h, d, k], RN[h, 1 - d, k]])

    def far3(h):
        for s in (1, -1):
            send(
                ("f3", h, s), T.at[h, turn(z, 2), here[O[h]], w(s)], RF3.at[h, w(s)],
                device("z", s),
            )

    def near3(h, s):
        send(
            ("n3", h, s), T.at[h, turn(z, s), here[O[h]], 1 - w(s)], RN3.at[h, w(s)],
            device("z", s),
        )

    def mid3(h, s):
        arrived("f3", h, s)
        add(turn(z, s), h, here[O[h]], w(s), [RF3[h, w(s)]])
        send(
            ("c3", h, s), T.at[h, turn(z, s), here[O[h]], w(s)], RC3.at[h, w(s)],
            device("z", s),
        )

    def end3(h):
        for s in (1, -1):
            arrived("n3", h, s)
            arrived("c3", h, s)
        for d in range(2):
            first = h * HALF + d * HALF // 2
            kg_o[0, first:first + HALF // 2, :] = (
                T[h, z, here[O[h]], d].astype(F32)
                + RC3[h, d].astype(F32)
                + RN3[h, 1 - d].astype(F32)
            )

    def keys(h, s):
        e = turn(here[E[h]], s)
        left = jnp.concatenate([X[h, turn(z, k), rows_of(e)] for k in range(SIDE)], axis=1)
        right = jnp.concatenate(
            [W[h, turn(z, k)].reshape(2 * BLK, W.shape[-1]) for k in range(SIDE)], axis=0
        )
        total = jnp.dot(left, right, preferred_element_type=F32)
        if s == 0:
            KA[h, s] = total
            return
        step = count // 2
        KS[h, s - 1] = total.astype(BF16)
        if s == 2:
            for t in (1, -1):
                send(
                    ("kf", h, t), KS.at[h, 1, pl.ds(w(t) * step, step)], KF.at[h, w(t)],
                    device(E[h], t),
                )
        else:
            t = 1 if s == 1 else -1
            KA[h, s] = total
            send(
                ("kn", h, t), KS.at[h, s - 1, pl.ds((1 - w(t)) * step, step)], KN.at[h, w(t)],
                device(E[h], t),
            )

    def keys_mid(h):
        step = count // 2
        for t in (1, -1):
            s, rows = t % SIDE, pl.ds(w(t) * step, step)
            arrived("kf", h, t)
            KS[h, s - 1, rows] = (KA[h, s, rows] + KF[h, w(t)].astype(F32)).astype(BF16)
            send(("kc", h, t), KS.at[h, s - 1, rows], KC.at[h, w(t)], device(E[h], t))

    def keys_end():
        step = count // 2
        for h in range(2):
            for t in (1, -1):
                arrived("kn", h, t)
        for d in range(2):
            rows = pl.ds(d * step, step)
            total = KA[0, 0, rows] + KA[1, 0, rows]
            for h in range(2):
                arrived("kc", h, 1 - 2 * d)
                total = total + KN[h, 1 - d].astype(F32) + KC[h, d].astype(F32)
            keys_o[0, rows] = total.astype(BF16)

    own = msv.shape[1]

    def outer_send():
        for c in got_outer:
            c.wait()
        for j in range(4):
            cols = slice(j * own, (j + 1) * own)
            corrected = (anv[:, cols].astype(F32) - lpv[:, cols].astype(F32)) + fbv[:, cols]
            pk[j] = corrected.astype(BF16)
        for k in (1, 2, 3):
            send(("pk", k), pk.at[lax.rem(r + k, 4)], RP.at[k - 1], peer(k))

    def outer_step():
        for c in got_state:
            c.wait()
        total = pk[r].astype(F32)
        for k in (1, 2, 3):
            arrived("pk", k)
            total = total + RP[k - 1].astype(F32)
        outer_grad = total / 4
        momentum_new = MU * mov[...] + outer_grad
        master_new = msv[...] - LR * (outer_grad + MU * momentum_new)
        mo_o[...] = momentum_new
        ms_o[...] = master_new
        AN[r] = master_new.astype(BF16)
        for k in (1, 2, 3):
            send(("an", k), AN.at[r], AN.at[r], peer(k))

    def outer_end():
        for k in (1, 2, 3):
            arrived("an", k)
        for j in range(4):
            an_o[:, j * own:(j + 1) * own] = AN[j]

    def both(step, *args):
        for h in range(2):
            step(h, *args)

    def terms(k):
        for h in range(2):
            term(h, k)
            far1(h, k)
            near1(h, k)

    w1()
    c1()
    w2(0)
    pack_all(2)
    share(2)
    pack_all(1)
    share(1)
    w2(1)
    w2(3)
    w2(2)
    c2()
    pack_all(3)
    share(3)
    w3(0)
    pack_all(0)
    share(0)
    outer_send()
    w3(1)
    c_end()
    both(shared, 2)
    terms(2)
    w3(3)
    both(shared, 1)
    terms(1)
    w3(2)
    both(shared, 3)
    terms(3)
    both(shared, 0)
    terms(0)
    outer_step()
    both(mid1, 2)
    both(mid1, 1)
    w_end()
    both(keys, 2)
    both(mid1, 3)
    both(mid1, 0)
    both(keys, 1)
    both(keys, 3)
    both(end1, 2)
    both(far3)
    both(end1, 1)
    both(near3, 1)
    both(end1, 3)
    both(near3, -1)
    both(keys_mid)
    both(mid3, 1)
    both(mid3, -1)
    both(keys, 0)
    outer_end()
    drain()
    both(end1, 0)
    both(end3)
    keys_end()
    drain()


def hand_over(*refs):
    sources, results, sems = refs[:5], refs[5:10], refs[10]
    copies = [pltpu.make_async_copy(a, b, sems.at[i]) for i, (a, b) in enumerate(zip(sources, results))]
    for c in copies:
        c.start()
    for c in copies:
        c.wait()


def on_device(lp, an, fb, ms, mo, tk, kw, kc):
    rows, width = an.shape
    own = ms.shape[1]
    tokens, fw = kc.shape[1], kc.shape[2]
    anywhere = pl.BlockSpec(memory_space=pl.ANY)
    out = [
        jax.ShapeDtypeStruct(ms.shape, F32),
        jax.ShapeDtypeStruct(mo.shape, F32),
        jax.ShapeDtypeStruct(an.shape, BF16),
        jax.ShapeDtypeStruct((1, tokens, fw), BF16),
        jax.ShapeDtypeStruct((1, BLK, fw), F32),
    ]
    v = pltpu.VMEM
    piece = (HALF // 2, fw)
    scratch = [
        v((2, SIDE, SIDE * tokens, SIDE * HALF), BF16),
        v((2, SIDE - 1, SIDE, tokens, SIDE * HALF), BF16),
        v((2, SIDE * tokens, fw), BF16),
        *[v((2, SIDE, SIDE, 2, *piece), BF16)] * 2,
        *[v((2, 2, SIDE, *piece), BF16)] * 3,
        *[v((2, 2, *piece), BF16)] * 3,
        v((2, SIDE, tokens, fw), F32),
        v((2, SIDE - 1, tokens, fw), BF16),
        *[v((2, 2, tokens // 2, fw), BF16)] * 3,
        v((tokens, width), BF16),
        v((rows, width), BF16),
        v((rows, width), BF16),
        v((rows, width), F32),
        v((rows, own), F32),
        v((rows, own), F32),
        v((4, rows, own), BF16),
        v((3, rows, own), BF16),
        v((4, rows, own), BF16),
        pltpu.SemaphoreType.DMA((MESSAGES,)),
        pltpu.SemaphoreType.DMA((MESSAGES,)),
        pltpu.SemaphoreType.DMA((27,)),
    ]
    done = pl.pallas_call(
        kernel,
        out_shape=[v(o.shape, o.dtype) for o in out],
        in_specs=[anywhere] * 8,
        out_specs=[pl.BlockSpec(memory_space=pltpu.VMEM)] * 5,
        scratch_shapes=scratch,
        compiler_params=pltpu.CompilerParams(
            collective_id=0, has_side_effects=True, vmem_limit_bytes=60 * 1024 * 1024
        ),
        cost_estimate=pl.CostEstimate(
            flops=4 * tokens * width * fw, bytes_accessed=12 * 1024 * 1024, transcendentals=0
        ),
    )(lp, an, fb, ms, mo, tk, kw, kc)
    return tuple(
        pl.pallas_call(
            hand_over,
            out_shape=out,
            in_specs=[pl.BlockSpec(memory_space=pltpu.VMEM)] * 5,
            out_specs=[anywhere] * 5,
            scratch_shapes=[pltpu.SemaphoreType.DMA((5,))],
        )(*[pltpu.with_memory_space_constraint(o, pltpu.VMEM) for o in done])
    )


def solution(mesh):
    in_specs = (
        P("replica", "fsdp", None),
        P("fsdp", None),
        P("replica", "fsdp", None),
        P("fsdp", "replica"),
        P("fsdp", "replica"),
        P("replica", "fsdp", None),
        P("replica", "fsdp", None),
        P("replica", "fsdp", None),
    )
    out_specs = (
        P("fsdp", "replica"),
        P("fsdp", "replica"),
        P("fsdp", None),
        P("replica", "fsdp", None),
        P("replica", "fsdp", None),
    )
    return jax.shard_map(
        on_device, mesh=mesh, in_specs=in_specs, out_specs=out_specs, check_vma=False
    )
```

```python
import functools

import jax
import jax.numpy as jnp
from jax import lax
from jax.experimental import pallas as pl
from jax.experimental.pallas import tpu as pltpu
from jax.sharding import PartitionSpec as P

LR = 0.7
MU = 0.9
MESH = pl.DeviceIdType.MESH
F32 = jnp.float32
BF16 = jnp.bfloat16
SIDE = 4
BLK = 128
HALF = BLK // 2
MESSAGES = 150


def kernel(
    lp, an, fb, ms, mo, tk, kw, kc,
    ms_o, mo_o, an_o, keys_o, kg_o,
    X, SP, C, W, T, RF, RN, RC, RF3, RN3, RC3, KA, KS, KF, KN, KC,
    tok, lpv, anv, fbv, msv, mov, pk, RP, AN,
    ssem, rsem, lsem,
):
    r = lax.axis_index("replica")
    f = lax.axis_index("fsdp")
    y, z, x = f // 16, (f // 4) % 4, f % 4
    here = {"y": y, "z": z, "x": x}
    E = ("x", "y")
    O = ("y", "x")
    count = tok.shape[0]

    def turn(v, s):
        return lax.rem(v + (s % SIDE), SIDE)

    def device(axis, s):
        c = dict(here)
        c[axis] = turn(c[axis], s)
        return (r, (c["y"] * SIDE + c["z"]) * SIDE + c["x"])

    def peer(k):
        return (lax.rem(r + k, 4), f)

    def rows_of(e):
        return pl.ds(pl.multiple_of(e * count, count), count)

    def w(s):
        return 0 if s == 1 else 1

    barrier = pltpu.get_barrier_semaphore()
    partners = (
        [device(axis, s) for axis in "xy" for s in (1, 2, 3)]
        + [device("z", s) for s in (1, 3)]
        + [peer(k) for k in (1, 2, 3)]
    )
    for partner in partners:
        pl.semaphore_signal(barrier, inc=1, device_id=partner, device_id_type=MESH)

    local = []

    def bring(src, dst):
        copy = pltpu.make_async_copy(src, dst, lsem.at[len(local)])
        copy.start()
        local.append(copy)
        return copy

    got_w = [
        bring(kw.at[0, pl.ds(h * HALF + d * HALF // 2, HALF // 2)], W.at[h, z, here[O[h]], d])
        for h in range(2) for d in range(2)
    ]
    got_c = [bring(kc.at[0], C.at[h, rows_of(here[E[h]])]) for h in range(2)]
    got_tok = {}
    for k in (2, 1, 3, 0):
        got_tok[k] = []
        for yy in range(SIDE):
            col = pl.multiple_of((yy * SIDE + turn(z, k)) * SIDE * BLK, SIDE * BLK)
            cols = pl.ds(col, SIDE * BLK)
            got_tok[k].append(bring(tk.at[0, :, cols], tok.at[:, cols]))
    got_outer = [bring(an, anv), bring(lp.at[0], lpv), bring(fb.at[0], fbv)]
    got_state = [bring(ms, msv), bring(mo, mov)]

    pl.semaphore_wait(barrier, len(partners))

    messages = []
    sent = {}

    def send(key, src, dst, to):
        i = len(messages)
        m = pltpu.make_async_remote_copy(
            src_ref=src, dst_ref=dst, send_sem=ssem.at[i], recv_sem=rsem.at[i],
            device_id=to, device_id_type=MESH,
        )
        m.start()
        messages.append(m)
        sent[key] = m

    def arrived(*key):
        sent[key].wait_recv()

    drained = []

    def drain():
        for m in messages[len(drained):]:
            m.wait_send()
            drained.append(m)

    def c1():
        for h in range(2):
            for s in (1, -1):
                send(("c1", h, s), kc.at[0], C.at[h, rows_of(here[E[h]])], device(E[h], s))

    def c2():
        for h in range(2):
            for s in (1, -1):
                arrived("c1", h, s)
                first = turn(here[E[h]], -s) * count + w(s) * (count // 2)
                src = C.at[h, pl.ds(pl.multiple_of(first, count // 2), count // 2)]
                send(("c2", h, s), src, src, device(E[h], s))

    def c_end():
        for c in got_c:
            c.wait()
        for h in range(2):
            for s in (1, -1):
                arrived("c2", h, s)

    def w1():
        for c in got_w:
            c.wait()
        for h in range(2):
            src = W.at[h, z, here[O[h]]]
            for s in (1, -1):
                send(("w1", h, s), src, src, device(O[h], s))

    def w1_on():
        for h in range(2):
            for s in (1, -1):
                arrived("w1", h, s)
                src = W.at[h, z, turn(here[O[h]], -s), w(s)]
                send(("w1", h, s, "on"), src, src, device(O[h], s))

    def w2(p):
        for h in range(2):
            if p == 2:
                for s in (1, -1):
                    arrived("w1", h, s, "on")
            src = W.at[h, z, turn(here[O[h]], p)]
            for s in (1, -1):
                send(("w2", h, p, s), src, src, device("z", s))

    def w3(p):
        for h in range(2):
            for s in (1, -1):
                arrived("w2", h, p, s)
                src = W.at[h, turn(z, -s), turn(here[O[h]], p), w(s)]
                send(("w3", h, p, s), src, src, device("z", s))

    def w_end():
        for h in range(2):
            for p in range(SIDE):
                for s in (1, -1):
                    arrived("w3", h, p, s)

    def pack(h, s, k):
        zz, e = turn(z, k), here[E[h]]
        ee = turn(e, s)
        for i in range(2):
            cols = []
            for oo in (2 * i, 2 * i + 1):
                yy, xx = (oo, ee) if h == 0 else (ee, oo)
                col = ((yy * SIDE + zz) * SIDE + xx) * BLK
                v = tok[:, pl.ds(pl.multiple_of(col, BLK), BLK)]
                cols.append(v[:, :HALF] if h == 0 else v[:, HALF:])
            both = jnp.concatenate(cols, axis=1)
            if s:
                SP[h, s - 1, k, :, i * BLK:(i + 1) * BLK] = both
            else:
                X[h, zz, rows_of(e), i * BLK:(i + 1) * BLK] = both

    def pack_all(k):
        for c in got_tok.pop(k):
            c.wait()
        for s in (2, 1, 3, 0):
            for h in range(2):
                pack(h, s, k)

    def share(k):
        for s in (2, 1, 3):
            for h in range(2):
                send(
                    ("x", h, s, k), SP.at[h, s - 1, k],
                    X.at[h, turn(z, k), rows_of(here[E[h]])], device(E[h], s),
                )

    def shared(h, k):
        for s in (1, 2, 3):
            arrived("x", h, s, k)

    def term(h, k):
        zz = turn(z, k)
        res = lax.dot_general(
            X[h, zz], C[h], (((0,), (0,)), ((), ())), preferred_element_type=F32
        ).astype(BF16)
        T[h, zz] = res.reshape(SIDE, 2, HALF // 2, res.shape[1])

    def far1(h, k):
        zz, o = turn(z, k), here[O[h]]
        for s in (1, -1):
            send(
                ("f1", h, k, s), T.at[h, zz, turn(o, 2), w(s)], RF.at[h, w(s), k],
                device(O[h], s),
            )

    def near1(h, k):
        zz, o = turn(z, k), here[O[h]]
        for s in (1, -1):
            send(
                ("n1", h, k, s), T.at[h, zz, turn(o, s), 1 - w(s)], RN.at[h, w(s), k],
                device(O[h], s),
            )

    def add(zz, h, o, d, others):
        total = T[h, zz, o, d].astype(F32)
        for part in others:
            total = total + part.astype(F32)
        T[h, zz, o, d] = total.astype(BF16)

    def mid1(h, k):
        zz, o = turn(z, k), here[O[h]]
        for s in (1, -1):
            arrived("f1", h, k, s)
            add(zz, h, turn(o, s), w(s), [RF[h, w(s), k]])
            send(
                ("c1", h, k, s), T.at[h, zz, turn(o, s), w(s)], RC.at[h, w(s), k],
                device(O[h], s),
            )

    def end1(h, k):
        zz, o = turn(z, k), here[O[h]]
        for s in (1, -1):
            arrived("n1", h, k, s)
            arrived("c1", h, k, s)
        for d in range(2):
            add(zz, h, o, d, [RC[h, d, k], RN[h, 1 - d, k]])

    def far3(h):
        for s in (1, -1):
            send(
                ("f3", h, s), T.at[h, turn(z, 2), here[O[h]], w(s)], RF3.at[h, w(s)],
                device("z", s),
            )

    def near3(h, s):
        send(
            ("n3", h, s), T.at[h, turn(z, s), here[O[h]], 1 - w(s)], RN3.at[h, w(s)],
            device("z", s),
        )

    def mid3(h, s):
        arrived("f3", h, s)
        add(turn(z, s), h, here[O[h]], w(s), [RF3[h, w(s)]])
        send(
            ("c3", h, s), T.at[h, turn(z, s), here[O[h]], w(s)], RC3.at[h, w(s)],
            device("z", s),
        )

    def end3(h):
        for s in (1, -1):
            arrived("n3", h, s)
            arrived("c3", h, s)
        for d in range(2):
            first = h * HALF + d * HALF // 2
            kg_o[0, first:first + HALF // 2, :] = (
                T[h, z, here[O[h]], d].astype(F32)
                + RC3[h, d].astype(F32)
                + RN3[h, 1 - d].astype(F32)
            )

    def keys(h, s):
        e = turn(here[E[h]], s)
        left = jnp.concatenate([X[h, turn(z, k), rows_of(e)] for k in range(SIDE)], axis=1)
        right = jnp.concatenate(
            [W[h, turn(z, k)].reshape(2 * BLK, W.shape[-1]) for k in range(SIDE)], axis=0
        )
        total = jnp.dot(left, right, preferred_element_type=F32)
        if s == 0:
            KA[h, s] = total
            return
        step = count // 2
        KS[h, s - 1] = total.astype(BF16)
        if s == 2:
            for t in (1, -1):
                send(
                    ("kf", h, t), KS.at[h, 1, pl.ds(w(t) * step, step)], KF.at[h, w(t)],
                    device(E[h], t),
                )
        else:
            t = 1 if s == 1 else -1
            KA[h, s] = total
            send(
                ("kn", h, t), KS.at[h, s - 1, pl.ds((1 - w(t)) * step, step)], KN.at[h, w(t)],
                device(E[h], t),
            )

    def keys_mid(h):
        step = count // 2
        for t in (1, -1):
            s, rows = t % SIDE, pl.ds(w(t) * step, step)
            arrived("kf", h, t)
            KS[h, s - 1, rows] = (KA[h, s, rows] + KF[h, w(t)].astype(F32)).astype(BF16)
            send(("kc", h, t), KS.at[h, s - 1, rows], KC.at[h, w(t)], device(E[h], t))

    def keys_end():
        step = count // 2
        for h in range(2):
            for t in (1, -1):
                arrived("kn", h, t)
        for d in range(2):
            rows = pl.ds(d * step, step)
            total = KA[0, 0, rows] + KA[1, 0, rows]
            for h in range(2):
                arrived("kc", h, 1 - 2 * d)
                total = total + KN[h, 1 - d].astype(F32) + KC[h, d].astype(F32)
            keys_o[0, rows] = total.astype(BF16)

    own = msv.shape[1]

    def outer_send():
        for c in got_outer:
            c.wait()
        for j in range(4):
            cols = slice(j * own, (j + 1) * own)
            corrected = (anv[:, cols].astype(F32) - lpv[:, cols].astype(F32)) + fbv[:, cols]
            pk[j] = corrected.astype(BF16)
        for k in (1, 2, 3):
            send(("pk", k), pk.at[lax.rem(r + k, 4)], RP.at[k - 1], peer(k))

    def outer_step():
        for c in got_state:
            c.wait()
        total = pk[r].astype(F32)
        for k in (1, 2, 3):
            arrived("pk", k)
            total = total + RP[k - 1].astype(F32)
        outer_grad = total / 4
        momentum_new = MU * mov[...] + outer_grad
        master_new = msv[...] - LR * (outer_grad + MU * momentum_new)
        mo_o[...] = momentum_new
        ms_o[...] = master_new
        AN[r] = master_new.astype(BF16)
        for k in (1, 2, 3):
            send(("an", k), AN.at[r], AN.at[r], peer(k))

    def outer_end():
        for k in (1, 2, 3):
            arrived("an", k)
        for j in range(4):
            an_o[:, j * own:(j + 1) * own] = AN[j]

    def both(step, *args):
        for h in range(2):
            step(h, *args)

    def terms(k):
        for h in range(2):
            term(h, k)
            far1(h, k)
            near1(h, k)

    w1()
    c1()
    w2(0)
    pack_all(2)
    share(2)
    pack_all(1)
    share(1)
    w1_on()
    w2(1)
    w2(3)
    c2()
    pack_all(3)
    share(3)
    w3(0)
    pack_all(0)
    share(0)
    w2(2)
    outer_send()
    w3(1)
    c_end()
    both(shared, 2)
    terms(2)
    w3(3)
    both(shared, 1)
    terms(1)
    w3(2)
    both(shared, 3)
    terms(3)
    both(shared, 0)
    terms(0)
    outer_step()
    both(mid1, 2)
    both(mid1, 1)
    w_end()
    both(keys, 2)
    both(mid1, 3)
    both(mid1, 0)
    both(keys, 1)
    both(keys, 3)
    both(end1, 2)
    both(far3)
    both(end1, 1)
    both(near3, 1)
    both(end1, 3)
    both(near3, -1)
    both(keys_mid)
    both(mid3, 1)
    both(mid3, -1)
    both(keys, 0)
    outer_end()
    drain()
    both(end1, 0)
    both(end3)
    keys_end()
    drain()


def hand_over(*refs):
    sources, results, sems = refs[:5], refs[5:10], refs[10]
    copies = [pltpu.make_async_copy(a, b, sems.at[i]) for i, (a, b) in enumerate(zip(sources, results))]
    for c in copies:
        c.start()
    for c in copies:
        c.wait()


def on_device(lp, an, fb, ms, mo, tk, kw, kc):
    rows, width = an.shape
    own = ms.shape[1]
    tokens, fw = kc.shape[1], kc.shape[2]
    anywhere = pl.BlockSpec(memory_space=pl.ANY)
    out = [
        jax.ShapeDtypeStruct(ms.shape, F32),
        jax.ShapeDtypeStruct(mo.shape, F32),
        jax.ShapeDtypeStruct(an.shape, BF16),
        jax.ShapeDtypeStruct((1, tokens, fw), BF16),
        jax.ShapeDtypeStruct((1, BLK, fw), F32),
    ]
    v = pltpu.VMEM
    piece = (HALF // 2, fw)
    scratch = [
        v((2, SIDE, SIDE * tokens, SIDE * HALF), BF16),
        v((2, SIDE - 1, SIDE, tokens, SIDE * HALF), BF16),
        v((2, SIDE * tokens, fw), BF16),
        *[v((2, SIDE, SIDE, 2, *piece), BF16)] * 2,
        *[v((2, 2, SIDE, *piece), BF16)] * 3,
        *[v((2, 2, *piece), BF16)] * 3,
        v((2, SIDE, tokens, fw), F32),
        v((2, SIDE - 1, tokens, fw), BF16),
        *[v((2, 2, tokens // 2, fw), BF16)] * 3,
        v((tokens, width), BF16),
        v((rows, width), BF16),
        v((rows, width), BF16),
        v((rows, width), F32),
        v((rows, own), F32),
        v((rows, own), F32),
        v((4, rows, own), BF16),
        v((3, rows, own), BF16),
        v((4, rows, own), BF16),
        pltpu.SemaphoreType.DMA((MESSAGES,)),
        pltpu.SemaphoreType.DMA((MESSAGES,)),
        pltpu.SemaphoreType.DMA((27,)),
    ]
    done = pl.pallas_call(
        kernel,
        out_shape=[v(o.shape, o.dtype) for o in out],
        in_specs=[anywhere] * 8,
        out_specs=[pl.BlockSpec(memory_space=pltpu.VMEM)] * 5,
        scratch_shapes=scratch,
        compiler_params=pltpu.CompilerParams(
            collective_id=0, has_side_effects=True, vmem_limit_bytes=60 * 1024 * 1024
        ),
        cost_estimate=pl.CostEstimate(
            flops=4 * tokens * width * fw, bytes_accessed=12 * 1024 * 1024, transcendentals=0
        ),
    )(lp, an, fb, ms, mo, tk, kw, kc)
    return tuple(
        pl.pallas_call(
            hand_over,
            out_shape=out,
            in_specs=[pl.BlockSpec(memory_space=pltpu.VMEM)] * 5,
            out_specs=[anywhere] * 5,
            scratch_shapes=[pltpu.SemaphoreType.DMA((5,))],
        )(*[pltpu.with_memory_space_constraint(o, pltpu.VMEM) for o in done])
    )


def solution(mesh):
    in_specs = (
        P("replica", "fsdp", None),
        P("fsdp", None),
        P("replica", "fsdp", None),
        P("fsdp", "replica"),
        P("fsdp", "replica"),
        P("replica", "fsdp", None),
        P("replica", "fsdp", None),
        P("replica", "fsdp", None),
    )
    out_specs = (
        P("fsdp", "replica"),
        P("fsdp", "replica"),
        P("fsdp", None),
        P("replica", "fsdp", None),
        P("replica", "fsdp", None),
    )
    return jax.shard_map(
        on_device, mesh=mesh, in_specs=in_specs, out_specs=out_specs, check_vma=False
    )
```

```python
import functools

import jax
import jax.numpy as jnp
from jax import lax
from jax.experimental import pallas as pl
from jax.experimental.pallas import tpu as pltpu
from jax.sharding import PartitionSpec as P

LR = 0.7
MU = 0.9
MESH = pl.DeviceIdType.MESH
F32 = jnp.float32
BF16 = jnp.bfloat16
SIDE = 4
BLK = 128
HALF = BLK // 2
MESSAGES = 150


def kernel(
    lp, an, fb, ms, mo, tk, kw, kc,
    ms_o, mo_o, an_o, keys_o, kg_o,
    X, SP, C, W, T, RF, RN, RC, RF3, RN3, RC3, KA, KS, KF, KN, KC,
    tok, lpv, anv, fbv, msv, mov, pk, RP, AN,
    ssem, rsem, lsem,
):
    r = lax.axis_index("replica")
    f = lax.axis_index("fsdp")
    y, z, x = f // 16, (f // 4) % 4, f % 4
    here = {"y": y, "z": z, "x": x}
    E = ("x", "y")
    O = ("y", "x")
    count = tok.shape[0]

    def turn(v, s):
        return lax.rem(v + (s % SIDE), SIDE)

    def device(axis, s):
        c = dict(here)
        c[axis] = turn(c[axis], s)
        return (r, (c["y"] * SIDE + c["z"]) * SIDE + c["x"])

    def peer(k):
        return (lax.rem(r + k, 4), f)

    def rows_of(e):
        return pl.ds(pl.multiple_of(e * count, count), count)

    def w(s):
        return 0 if s == 1 else 1

    barrier = pltpu.get_barrier_semaphore()
    partners = (
        [device(axis, s) for axis in "xy" for s in (1, 2, 3)]
        + [device("z", s) for s in (1, 3)]
        + [peer(k) for k in (1, 2, 3)]
    )
    for partner in partners:
        pl.semaphore_signal(barrier, inc=1, device_id=partner, device_id_type=MESH)

    local = []

    def bring(src, dst):
        copy = pltpu.make_async_copy(src, dst, lsem.at[len(local)])
        copy.start()
        local.append(copy)
        return copy

    got_w = [
        bring(kw.at[0, pl.ds(h * HALF + d * HALF // 2, HALF // 2)], W.at[h, z, here[O[h]], d])
        for h in range(2) for d in range(2)
    ]
    got_c = [bring(kc.at[0], C.at[h, rows_of(here[E[h]])]) for h in range(2)]
    got_tok = {}
    for k in (2, 1, 3, 0):
        got_tok[k] = []
        for yy in range(SIDE):
            col = pl.multiple_of((yy * SIDE + turn(z, k)) * SIDE * BLK, SIDE * BLK)
            cols = pl.ds(col, SIDE * BLK)
            got_tok[k].append(bring(tk.at[0, :, cols], tok.at[:, cols]))
    got_outer = [bring(an, anv), bring(lp.at[0], lpv), bring(fb.at[0], fbv)]
    got_state = [bring(ms, msv), bring(mo, mov)]

    pl.semaphore_wait(barrier, len(partners))

    messages = []
    sent = {}

    def send(key, src, dst, to):
        i = len(messages)
        m = pltpu.make_async_remote_copy(
            src_ref=src, dst_ref=dst, send_sem=ssem.at[i], recv_sem=rsem.at[i],
            device_id=to, device_id_type=MESH,
        )
        m.start()
        messages.append(m)
        sent[key] = m

    def arrived(*key):
        sent[key].wait_recv()

    drained = []

    def drain():
        for m in messages[len(drained):]:
            m.wait_send()
            drained.append(m)

    def c1():
        for h in range(2):
            for s in (1, -1):
                send(("c1", h, s), kc.at[0], C.at[h, rows_of(here[E[h]])], device(E[h], s))

    def c2():
        for h in range(2):
            for s in (1, -1):
                arrived("c1", h, s)
                first = turn(here[E[h]], -s) * count + w(s) * (count // 2)
                src = C.at[h, pl.ds(pl.multiple_of(first, count // 2), count // 2)]
                send(("c2", h, s), src, src, device(E[h], s))

    def c_end():
        for c in got_c:
            c.wait()
        for h in range(2):
            for s in (1, -1):
                arrived("c2", h, s)

    def w1():
        for c in got_w:
            c.wait()
        for h in range(2):
            src = W.at[h, z, here[O[h]]]
            for s in (1, -1):
                send(("w1", h, s), src, src, device(O[h], s))

    def w1_on():
        for h in range(2):
            for s in (1, -1):
                arrived("w1", h, s)
                src = W.at[h, z, turn(here[O[h]], -s), w(s)]
                send(("w1", h, s, "on"), src, src, device(O[h], s))

    def w2(p):
        for h in range(2):
            if p == 2:
                for s in (1, -1):
                    arrived("w1", h, s, "on")
            src = W.at[h, z, turn(here[O[h]], p)]
            for s in (1, -1):
                send(("w2", h, p, s), src, src, device("z", s))

    def w3(p):
        for h in range(2):
            for s in (1, -1):
                arrived("w2", h, p, s)
                src = W.at[h, turn(z, -s), turn(here[O[h]], p), w(s)]
                send(("w3", h, p, s), src, src, device("z", s))

    def w_end():
        for h in range(2):
            for p in range(SIDE):
                for s in (1, -1):
                    arrived("w3", h, p, s)

    def pack(h, s, k):
        zz, e = turn(z, k), here[E[h]]
        ee = turn(e, s)
        for i in range(2):
            cols = []
            for oo in (2 * i, 2 * i + 1):
                yy, xx = (oo, ee) if h == 0 else (ee, oo)
                col = ((yy * SIDE + zz) * SIDE + xx) * BLK
                v = tok[:, pl.ds(pl.multiple_of(col, BLK), BLK)]
                cols.append(v[:, :HALF] if h == 0 else v[:, HALF:])
            both = jnp.concatenate(cols, axis=1)
            if s:
                SP[h, s - 1, k, :, i * BLK:(i + 1) * BLK] = both
            else:
                X[h, zz, rows_of(e), i * BLK:(i + 1) * BLK] = both

    def pack_all(k):
        for c in got_tok.pop(k):
            c.wait()
        for s in (2, 1, 3, 0):
            for h in range(2):
                pack(h, s, k)

    def share(k):
        for s in (2, 1, 3):
            for h in range(2):
                send(
                    ("x", h, s, k), SP.at[h, s - 1, k],
                    X.at[h, turn(z, k), rows_of(here[E[h]])], device(E[h], s),
                )

    def shared(h, k):
        for s in (1, 2, 3):
            arrived("x", h, s, k)

    def term(h, k):
        zz = turn(z, k)
        res = lax.dot_general(
            X[h, zz], C[h], (((0,), (0,)), ((), ())), preferred_element_type=F32
        ).astype(BF16)
        T[h, zz] = res.reshape(SIDE, 2, HALF // 2, res.shape[1])

    def far1(h, k):
        zz, o = turn(z, k), here[O[h]]
        for s in (1, -1):
            send(
                ("f1", h, k, s), T.at[h, zz, turn(o, 2), w(s)], RF.at[h, w(s), k],
                device(O[h], s),
            )

    def near1(h, k):
        zz, o = turn(z, k), here[O[h]]
        for s in (1, -1):
            send(
                ("n1", h, k, s), T.at[h, zz, turn(o, s), 1 - w(s)], RN.at[h, w(s), k],
                device(O[h], s),
            )

    def add(zz, h, o, d, others):
        total = T[h, zz, o, d].astype(F32)
        for part in others:
            total = total + part.astype(F32)
        T[h, zz, o, d] = total.astype(BF16)

    def mid1(h, k):
        zz, o = turn(z, k), here[O[h]]
        for s in (1, -1):
            arrived("f1", h, k, s)
            add(zz, h, turn(o, s), w(s), [RF[h, w(s), k]])
            send(
                ("c1", h, k, s), T.at[h, zz, turn(o, s), w(s)], RC.at[h, w(s), k],
                device(O[h], s),
            )

    def end1(h, k):
        zz, o = turn(z, k), here[O[h]]
        for s in (1, -1):
            arrived("n1", h, k, s)
            arrived("c1", h, k, s)
        for d in range(2):
            add(zz, h, o, d, [RC[h, d, k], RN[h, 1 - d, k]])

    def far3(h):
        for s in (1, -1):
            send(
                ("f3", h, s), T.at[h, turn(z, 2), here[O[h]], w(s)], RF3.at[h, w(s)],
                device("z", s),
            )

    def near3(h, s):
        send(
            ("n3", h, s), T.at[h, turn(z, s), here[O[h]], 1 - w(s)], RN3.at[h, w(s)],
            device("z", s),
        )

    def mid3(h, s):
        arrived("f3", h, s)
        add(turn(z, s), h, here[O[h]], w(s), [RF3[h, w(s)]])
        send(
            ("c3", h, s), T.at[h, turn(z, s), here[O[h]], w(s)], RC3.at[h, w(s)],
            device("z", s),
        )

    def end3(h):
        for s in (1, -1):
            arrived("n3", h, s)
            arrived("c3", h, s)
        for d in range(2):
            first = h * HALF + d * HALF // 2
            kg_o[0, first:first + HALF // 2, :] = (
                T[h, z, here[O[h]], d].astype(F32)
                + RC3[h, d].astype(F32)
                + RN3[h, 1 - d].astype(F32)
            )

    def keys(h, s):
        e = turn(here[E[h]], s)
        left = jnp.concatenate([X[h, turn(z, k), rows_of(e)] for k in range(SIDE)], axis=1)
        right = jnp.concatenate(
            [W[h, turn(z, k)].reshape(2 * BLK, W.shape[-1]) for k in range(SIDE)], axis=0
        )
        total = jnp.dot(left, right, preferred_element_type=F32)
        if s == 0:
            KA[h, s] = total
            return
        step = count // 2
        KS[h, s - 1] = total.astype(BF16)
        if s == 2:
            for t in (1, -1):
                send(
                    ("kf", h, t), KS.at[h, 1, pl.ds(w(t) * step, step)], KF.at[h, w(t)],
                    device(E[h], t),
                )
        else:
            t = 1 if s == 1 else -1
            KA[h, s] = total
            send(
                ("kn", h, t), KS.at[h, s - 1, pl.ds((1 - w(t)) * step, step)], KN.at[h, w(t)],
                device(E[h], t),
            )

    def keys_mid(h):
        step = count // 2
        for t in (1, -1):
            s, rows = t % SIDE, pl.ds(w(t) * step, step)
            arrived("kf", h, t)
            KS[h, s - 1, rows] = (KA[h, s, rows] + KF[h, w(t)].astype(F32)).astype(BF16)
            send(("kc", h, t), KS.at[h, s - 1, rows], KC.at[h, w(t)], device(E[h], t))

    def keys_end():
        step = count // 2
        for h in range(2):
            for t in (1, -1):
                arrived("kn", h, t)
        for d in range(2):
            rows = pl.ds(d * step, step)
            total = KA[0, 0, rows] + KA[1, 0, rows]
            for h in range(2):
                arrived("kc", h, 1 - 2 * d)
                total = total + KN[h, 1 - d].astype(F32) + KC[h, d].astype(F32)
            keys_o[0, rows] = total.astype(BF16)

    own = msv.shape[1]

    def outer_send():
        for c in got_outer:
            c.wait()
        for j in range(4):
            cols = slice(j * own, (j + 1) * own)
            corrected = (anv[:, cols].astype(F32) - lpv[:, cols].astype(F32)) + fbv[:, cols]
            pk[j] = corrected.astype(BF16)
        for k in (1, 2, 3):
            send(("pk", k), pk.at[lax.rem(r + k, 4)], RP.at[k - 1], peer(k))

    def outer_step():
        for c in got_state:
            c.wait()
        total = pk[r].astype(F32)
        for k in (1, 2, 3):
            arrived("pk", k)
            total = total + RP[k - 1].astype(F32)
        outer_grad = total / 4
        momentum_new = MU * mov[...] + outer_grad
        master_new = msv[...] - LR * (outer_grad + MU * momentum_new)
        mo_o[...] = momentum_new
        ms_o[...] = master_new
        AN[r] = master_new.astype(BF16)
        for k in (1, 2, 3):
            send(("an", k), AN.at[r], AN.at[r], peer(k))

    def outer_end():
        for k in (1, 2, 3):
            arrived("an", k)
        for j in range(4):
            an_o[:, j * own:(j + 1) * own] = AN[j]

    def both(step, *args):
        for h in range(2):
            step(h, *args)

    def terms(k):
        for h in range(2):
            term(h, k)
            far1(h, k)
            near1(h, k)

    w1()
    c1()
    w2(0)
    pack_all(2)
    share(2)
    pack_all(1)
    share(1)
    w1_on()
    w2(1)
    w2(3)
    c2()
    pack_all(3)
    share(3)
    w3(0)
    pack_all(0)
    share(0)
    w2(2)
    outer_send()
    w3(1)
    c_end()
    both(shared, 2)
    terms(2)
    w3(3)
    both(shared, 1)
    terms(1)
    w3(2)
    both(shared, 3)
    terms(3)
    both(shared, 0)
    terms(0)
    outer_step()
    both(mid1, 2)
    both(mid1, 1)
    w_end()
    both(keys, 2)
    both(mid1, 3)
    both(mid1, 0)
    both(keys, 1)
    both(keys, 3)
    both(end1, 2)
    both(far3)
    both(end1, 1)
    both(near3, 1)
    both(end1, 3)
    both(near3, -1)
    both(keys_mid)
    both(mid3, 1)
    both(mid3, -1)
    both(keys, 0)
    both(end1, 0)
    both(end3)
    outer_end()
    drain()
    keys_end()
    drain()


def hand_over(*refs):
    sources, results, sems = refs[:5], refs[5:10], refs[10]
    copies = [pltpu.make_async_copy(a, b, sems.at[i]) for i, (a, b) in enumerate(zip(sources, results))]
    for c in copies:
        c.start()
    for c in copies:
        c.wait()


def on_device(lp, an, fb, ms, mo, tk, kw, kc):
    rows, width = an.shape
    own = ms.shape[1]
    tokens, fw = kc.shape[1], kc.shape[2]
    anywhere = pl.BlockSpec(memory_space=pl.ANY)
    out = [
        jax.ShapeDtypeStruct(ms.shape, F32),
        jax.ShapeDtypeStruct(mo.shape, F32),
        jax.ShapeDtypeStruct(an.shape, BF16),
        jax.ShapeDtypeStruct((1, tokens, fw), BF16),
        jax.ShapeDtypeStruct((1, BLK, fw), F32),
    ]
    v = pltpu.VMEM
    piece = (HALF // 2, fw)
    scratch = [
        v((2, SIDE, SIDE * tokens, SIDE * HALF), BF16),
        v((2, SIDE - 1, SIDE, tokens, SIDE * HALF), BF16),
        v((2, SIDE * tokens, fw), BF16),
        *[v((2, SIDE, SIDE, 2, *piece), BF16)] * 2,
        *[v((2, 2, SIDE, *piece), BF16)] * 3,
        *[v((2, 2, *piece), BF16)] * 3,
        v((2, SIDE, tokens, fw), F32),
        v((2, SIDE - 1, tokens, fw), BF16),
        *[v((2, 2, tokens // 2, fw), BF16)] * 3,
        v((tokens, width), BF16),
        v((rows, width), BF16),
        v((rows, width), BF16),
        v((rows, width), F32),
        v((rows, own), F32),
        v((rows, own), F32),
        v((4, rows, own), BF16),
        v((3, rows, own), BF16),
        v((4, rows, own), BF16),
        pltpu.SemaphoreType.DMA((MESSAGES,)),
        pltpu.SemaphoreType.DMA((MESSAGES,)),
        pltpu.SemaphoreType.DMA((27,)),
    ]
    done = pl.pallas_call(
        kernel,
        out_shape=[v(o.shape, o.dtype) for o in out],
        in_specs=[anywhere] * 8,
        out_specs=[pl.BlockSpec(memory_space=pltpu.VMEM)] * 5,
        scratch_shapes=scratch,
        compiler_params=pltpu.CompilerParams(
            collective_id=0, has_side_effects=True, vmem_limit_bytes=60 * 1024 * 1024
        ),
        cost_estimate=pl.CostEstimate(
            flops=4 * tokens * width * fw, bytes_accessed=12 * 1024 * 1024, transcendentals=0
        ),
    )(lp, an, fb, ms, mo, tk, kw, kc)
    return tuple(
        pl.pallas_call(
            hand_over,
            out_shape=out,
            in_specs=[pl.BlockSpec(memory_space=pltpu.VMEM)] * 5,
            out_specs=[anywhere] * 5,
            scratch_shapes=[pltpu.SemaphoreType.DMA((5,))],
        )(*[pltpu.with_memory_space_constraint(o, pltpu.VMEM) for o in done])
    )


def solution(mesh):
    in_specs = (
        P("replica", "fsdp", None),
        P("fsdp", None),
        P("replica", "fsdp", None),
        P("fsdp", "replica"),
        P("fsdp", "replica"),
        P("replica", "fsdp", None),
        P("replica", "fsdp", None),
        P("replica", "fsdp", None),
    )
    out_specs = (
        P("fsdp", "replica"),
        P("fsdp", "replica"),
        P("fsdp", None),
        P("replica", "fsdp", None),
        P("replica", "fsdp", None),
    )
    return jax.shard_map(
        on_device, mesh=mesh, in_specs=in_specs, out_specs=out_specs, check_vma=False
    )
```
